512 devices in a mesh: tile: 64 (over x, z), rep: 8 (over y, core).
Axes of the slice: x: 4, y: 4, z: 16, core: 2. Of those that a mesh axis runs over, the one named last changes fastest.
Arguments:
- owner: int32 [262144, 1], P(('tile', 'rep')), may hold values from 0 to 63; in each aligned block of 512 rows (0 to 511, 512 to 1023, ...) at most 24 rows name the same one
- tile_local: int32 [262144], P(('tile', 'rep')), may hold values from 0 to 15
- anchor: int32 [262144], P(('tile', 'rep')), may hold values from 0 to 224
- frac_x: int32 [262144], P(('tile', 'rep')), may hold values from 0 to 255
- frac_y: int32 [262144], P(('tile', 'rep')), may hold values from 0 to 255
- label: int32 [262144], P(('tile', 'rep')), may hold values 0 or 1
- raster: bfloat16 [1024, 64, 256], P('tile'), may hold values from -6 to 6
- beta: float32 [512], replicated, may hold values from -0.9 to 0.9
- smooth: float32 [64], replicated, may hold values from 0.002 to 0.05
Outputs:
- beta_new: float32 [512], replicated
- eta_new: float32 [262144], P(('tile', 'rep'))
The draws below stay inside these ranges and needn't reach their ends.
Inputs may be any that keep to these rules, and one draw needn't show every extreme that they name: Among the 512 fixes of one device no owner is named more than 24 times, and 24 is reached for some owner. The square's lower-left cell is row anchor // 15 and column anchor mod 15 of the tile, so the whole square lies inside the tile.
All inputs are finite; a program needn't handle non-finite values. No bound on the sum of `label` on one device may be relied on, other than what follows from the above.
Results may differ from the reference program's by a relative error of at most 0.0033.
Values may be sent and summed in bfloat16 or wider, within the bound.
A program may use at most 128 MiB of HBM per device.

```python
import math
import jax
import jax.numpy as jnp
import numpy as np
from jax import lax

LAYERS = 64
SPLINES = 8
TOK_DEV = 512
TILES_DEV = 16
BASIS = 512
CAP = 24
TOKENS = 262144
TILES = 1024
N_TILE = 64


def touch_ends(drawn, rng, least, top_value):
    extent = drawn.shape
    spot = [jax.random.randint(jax.random.fold_in(rng, axis), (), 0, extent[axis]) for axis in range(len(extent))]
    drawn = drawn.at[tuple(spot)].set(least)
    longest = extent.index(max(extent))
    spot[longest] = (spot[longest] + 1) % extent[longest]
    return drawn.at[tuple(spot)].set(top_value)


def steps_of(key, extent, cuts, low, top_value):
    gain = 1.0
    for axis_at, blocks in cuts:
        steps = jax.random.uniform(jax.random.fold_in(jax.random.fold_in(key, 6), axis_at), (blocks,), jnp.float32, low / len(cuts), top_value / len(cuts))
        gain = gain * jnp.repeat(jnp.exp(steps), extent[axis_at] // blocks).reshape((-1,) + (1,) * (len(extent) - 1 - axis_at))
    return gain


def routed_block(rng, own, number, rows, number_of, top, most, slope):
    order = jax.random.permutation(rng, number_of)
    crowded, common = portions_of(number_of, rows * top, most, slope, True), portions_of(number_of, rows * top, most, slope, False)
    places = jnp.arange(number_of)

    def named(tallies, turn):
        used = int((tallies > 0).sum())
        fixed = max(1, used // 4)
        shifted = fixed + (places - fixed + turn * (used - fixed)) % max(1, number_of - fixed)
        return jnp.zeros((number_of,), jnp.int32).at[order[jnp.where(places < fixed, places, shifted)]].set(jnp.asarray(tallies, jnp.int32))

    tallies = jnp.where(number % 4 == 0, named(crowded, number // 4), named(common, number - number // 4 - 1))
    mixed = jax.random.permutation(jax.random.fold_in(own, 3), number_of)
    donor, sink = mixed[0:number_of // 2 * 2:2], mixed[1:number_of // 2 * 2:2]
    slack = jnp.minimum(tallies[donor] - 1, most - tallies[sink]) // 2
    slack = jnp.where((donor == order[0]) | (sink == order[0]) | (tallies[sink] == 0), 0, jnp.maximum(slack, 0))
    shifted = jax.random.randint(jax.random.fold_in(own, 4), (number_of // 2,), 0, 1 << 20) % (slack + 1)
    tallies = tallies.at[donor].add(-shifted).at[sink].add(shifted)
    items = jnp.searchsorted(jnp.cumsum(tallies), jnp.arange(rows * top), side="right").astype(jnp.int32)
    listing = items.reshape(top, rows).T
    listing = listing[jax.random.permutation(jax.random.fold_in(own, 1), rows)]
    turn = jax.random.randint(jax.random.fold_in(own, 2), (rows, 1), 0, top)
    return jnp.take_along_axis(listing, (jnp.arange(top)[None, :] + turn) % top, axis=1)


def portions_of(amount, total, reach, skew, full):
    loads = [(1 << 20) // math.isqrt(rank ** skew) + 1 for rank in range(1, amount + 1)]
    largest = reach if full else min(reach, max(-(-total // amount), total * loads[0] // sum(loads)))
    least = 1 if total - largest >= amount - 1 else 0
    counts, surplus = [largest] + [least] * (amount - 1), total - largest - least * (amount - 1)
    while surplus > 0:
        movable = [i for i in range(1, amount) if counts[i] < largest] or [i for i in range(1, amount) if counts[i] < reach]
        whole, budget = sum([loads[i] for i in movable]), surplus
        for i in movable:
            extra = min(reach - counts[i], max(1, budget * loads[i] // whole), surplus)
            counts[i] = counts[i] + extra
            surplus = surplus - extra
    return np.array(counts)


def bell_draw(rng, extent, scale, bound, cuts=(), kind=jnp.bfloat16):
    result = scale * jax.random.normal(rng, extent, jnp.float32)
    if cuts:
        result = result * steps_of(rng, extent, cuts, -0.22, 0.18)
    return jnp.clip(result, -bound, bound).astype(kind)


def setup_inputs(seed: int = 0) -> dict:
    key_of = jax.random.split(jax.random.key(seed), 10)
    owner_keys = jax.random.split(jax.random.fold_in(key_of[0], 1), TOKENS // TOK_DEV)
    owner_turns = jax.random.permutation(jax.random.fold_in(key_of[0], 3), TOKENS // TOK_DEV)
    owner = jax.vmap(lambda own, number: routed_block(jax.random.fold_in(key_of[0], 2), own, number, TOK_DEV, N_TILE, 1, CAP, 2))(owner_keys, owner_turns).reshape((TOKENS, 1))
    tile_local = touch_ends(jax.random.randint(key_of[1], (TOKENS,), 0, TILES_DEV), jax.random.fold_in(key_of[1], 1), 0, TILES_DEV - 1).astype(jnp.int32)
    anchor = touch_ends(jax.random.randint(key_of[2], (TOKENS,), 0, 225), jax.random.fold_in(key_of[2], 1), 0, 224).astype(jnp.int32)
    frac_x = touch_ends(jax.random.randint(key_of[3], (TOKENS,), 0, 256), jax.random.fold_in(key_of[3], 1), 0, 255).astype(jnp.int32)
    frac_y = touch_ends(jax.random.randint(key_of[4], (TOKENS,), 0, 256), jax.random.fold_in(key_of[4], 1), 0, 255).astype(jnp.int32)
    label = touch_ends((jax.random.randint(key_of[5], (TOKENS,), 0, 3) < 1).astype(jnp.int32), jax.random.fold_in(key_of[5], 1), 0, 1)
    raster = bell_draw(key_of[6], (TILES, LAYERS, 256), 1.0, 6.0, ((0, 64),))
    beta = bell_draw(key_of[7], (BASIS,), 0.15, 0.9, (), jnp.float32)
    smooth = jnp.clip(jnp.exp(jax.random.uniform(key_of[8], (LAYERS,), jnp.float32, math.log(0.002), math.log(0.05))), 0.002, 0.05)
    return dict(owner=owner, tile_local=tile_local, anchor=anchor, frac_x=frac_x, frac_y=frac_y, label=label, raster=raster, beta=beta, smooth=smooth)


RIDGE = 0.002

def interpolate(raster, tiles, anchors, frac_x, frac_y):
    row_id = anchors // 15
    corner = row_id * 16 + (anchors - row_id * 15)
    weight_x = frac_x.astype(jnp.float32)
    weight_y = frac_y.astype(jnp.float32)
    lower_left = raster[tiles, :, corner].astype(jnp.float32)
    lower_right = raster[tiles, :, corner + 1].astype(jnp.float32)
    upper_left = raster[tiles, :, corner + 16].astype(jnp.float32)
    upper_right = raster[tiles, :, corner + 17].astype(jnp.float32)
    total = ((256.0 - weight_x) * (256.0 - weight_y))[..., None] * lower_left
    total = total + (weight_x * (256.0 - weight_y))[..., None] * lower_right
    total = total + ((256.0 - weight_x) * weight_y)[..., None] * upper_left
    total = total + (weight_x * weight_y)[..., None] * upper_right
    return total / 65536.0

def expand(values):
    knots = 0.5 * (jnp.arange(SPLINES, dtype=jnp.float32) - (SPLINES - 1) / 2.0)
    bumps = jnp.maximum(1.0 - jnp.abs(values[..., None] - knots) / 0.75, 0.0) ** 3
    return bumps.reshape(values.shape[:-1] + (values.shape[-1] * SPLINES,)).astype(jnp.bfloat16)

def normal_terms(rows, beta, outcome, live):
    rows_wide = rows.astype(jnp.float32)
    eta = jnp.dot(rows_wide, beta, precision=lax.Precision.HIGHEST)
    prob = jax.nn.sigmoid(eta)
    weight = prob * (1.0 - prob) * live
    scaled = (jnp.sqrt(weight)[:, None] * rows_wide).astype(jnp.bfloat16)
    gram = jnp.dot(scaled.T.astype(jnp.float32), scaled.astype(jnp.float32), preferred_element_type=jnp.float32)
    resid = weight * eta + (outcome - prob) * live
    target = jnp.dot(resid, rows_wide, precision=lax.Precision.HIGHEST)
    return (gram, target)

def penalty(smooth):
    first = jnp.arange(SPLINES - 2)[:, None]
    cols = jnp.arange(SPLINES)[None, :]
    second = (cols == first).astype(jnp.float32) - 2.0 * (cols == first + 1).astype(jnp.float32) + (cols == first + 2).astype(jnp.float32)
    inner = jnp.dot(second.T, second, precision=lax.Precision.HIGHEST)
    layers = smooth.shape[0]
    blocks = jnp.eye(layers, dtype=jnp.float32)[:, None, :, None] * smooth[:, None, None, None] * inner[None, :, None, :]
    return blocks.reshape(layers * SPLINES, layers * SPLINES)

def solve_step(gram, target, smooth, count):
    system = gram / count + penalty(smooth) + RIDGE * jnp.eye(gram.shape[0], dtype=jnp.float32)
    factor = jnp.linalg.cholesky(system)
    return jax.scipy.linalg.cho_solve((factor, True), target / count)

def reference(owner, tile_local, anchor, frac_x, frac_y, label, raster, beta, smooth):
    tiles = owner[:, 0] * TILES_DEV + tile_local
    blocks = TOKENS // TOK_DEV
    pieces = (tiles.reshape(blocks, TOK_DEV), anchor.reshape(blocks, TOK_DEV), frac_x.reshape(blocks, TOK_DEV), frac_y.reshape(blocks, TOK_DEV), label.reshape(blocks, TOK_DEV))
    live = jnp.ones((TOK_DEV,), jnp.float32)

    def accumulate(carry, piece):
        rows = expand(interpolate(raster, piece[0], piece[1], piece[2], piece[3]))
        gram, target = normal_terms(rows, beta, piece[4].astype(jnp.float32), live)
        return ((carry[0] + gram, carry[1] + target), None)
    start = (jnp.zeros((BASIS, BASIS), jnp.float32), jnp.zeros((BASIS,), jnp.float32))
    (gram, target), _ = lax.scan(accumulate, start, pieces)
    beta_new = solve_step(gram, target, smooth, float(TOKENS))

    def predict(carry, piece):
        rows = expand(interpolate(raster, piece[0], piece[1], piece[2], piece[3]))
        return (carry, jnp.dot(rows.astype(jnp.float32), beta_new, precision=lax.Precision.HIGHEST))
    _, eta_new = lax.scan(predict, jnp.zeros((), jnp.float32), pieces)
    return (beta_new, eta_new.reshape(TOKENS))
```

```python
import functools

import jax
import jax.numpy as jnp
from jax import lax
from jax.experimental import pallas as pl
from jax.experimental.pallas import tpu as pltpu
from jax.sharding import PartitionSpec as P

SPLINES = 8
RIDGE = 0.002
LAYERS = 64
BASIS = 512
FIXES = 512
SLOTS = 24
OWNERS = 64
PLANE = 16
DEEP = 16
ROWS = 48
MESH = pl.DeviceIdType.MESH
HIGHEST = lax.Precision.HIGHEST
VMEM = pl.BlockSpec(memory_space=pltpu.VMEM)
SMEM = pl.BlockSpec(memory_space=pltpu.SMEM)
LIMIT = 48 * 1024 * 1024
BLOCKS = [(i, j) for i in range(4) for j in range(i, 4)]
NT = (((1,), (1,)), ((), ()))
TN = (((0,), (0,)), ((), ()))


def dot(a, b, dims=(((1,), (0,)), ((), ())), precision=None):
    return lax.dot_general(a, b, dims, precision=precision, preferred_element_type=jnp.float32)


def iota(shape, axis):
    return lax.broadcasted_iota(jnp.int32, shape, axis)


def thirds(x):
    high = x.astype(jnp.bfloat16)
    rest = x - high.astype(jnp.float32)
    mid = rest.astype(jnp.bfloat16)
    low = (rest - mid.astype(jnp.float32)).astype(jnp.bfloat16)
    return high, mid, low


def stacked_thirds(x):
    high, mid, low = thirds(x)
    row = iota((16, x.shape[1]), 0)
    wide = lambda part: jnp.broadcast_to(part.astype(jnp.float32), row.shape)
    parts = jnp.where(row == 0, wide(high), jnp.where(row == 1, wide(mid), jnp.where(row == 2, wide(low), 0.0)))
    return parts.astype(jnp.bfloat16)


def position():
    return lax.axis_index("tile"), lax.axis_index("rep")


def request_rows(owner, local, anchor, frac_x, frac_y, label):
    named = (iota((OWNERS, FIXES), 0) == owner).astype(jnp.float32)
    named_b = named.astype(jnp.bfloat16)
    earlier = (iota((FIXES, FIXES), 0) < iota((FIXES, FIXES), 1)).astype(jnp.float32).astype(jnp.bfloat16)
    before = dot(named_b, earlier)
    slot = jnp.sum(before * named, axis=0, keepdims=True)
    at = iota((SLOTS, FIXES), 0).astype(jnp.float32) == slot
    fields = [field.astype(jnp.float32) for field in (local, anchor, frac_x, frac_y, label + 1)]
    spread = [jnp.where(at, field, 0.0) for field in fields] + [jnp.zeros((8, FIXES), jnp.float32)]
    spread = jnp.concatenate(spread, axis=0).astype(jnp.bfloat16)
    return dot(named_b, spread, NT), slot


def greet_tile(barrier, tile, rep):
    def greet(step, _):
        pl.semaphore_signal(barrier, inc=1, device_id=(lax.rem(tile + step, OWNERS), rep), device_id_type=MESH)
        return 0

    lax.fori_loop(1, OWNERS, greet, 0)


def exchange(tile, rep, out, came, send_sem, recv_sem):
    def copy(peer, slot):
        return pltpu.make_async_remote_copy(
            src_ref=out.at[peer], dst_ref=came.at[slot], send_sem=send_sem.at[peer], recv_sem=recv_sem.at[slot],
            device_id=(peer, rep), device_id_type=MESH)

    def begin(step, _):
        copy(lax.rem(tile + step, OWNERS), tile).start()
        return 0

    def finish(step, _):
        peer = lax.rem(tile + step, OWNERS)
        copy(peer, peer).wait_recv()
        copy(peer, peer).wait_send()
        return 0

    lax.fori_loop(1, OWNERS, begin, 0)
    came[tile] = out[tile]
    lax.fori_loop(1, OWNERS, finish, 0)


def request_kernel(owner, local, anchor, frac_x, frac_y, label, codes, slot_out, out, came, send_sem, recv_sem):
    tile, rep = position()
    barrier = pltpu.get_barrier_semaphore()
    greet_tile(barrier, tile, rep)
    message, slot = request_rows(owner[...], local[...], anchor[...], frac_x[...], frac_y[...], label[...])
    slot_out[...] = slot
    for k in range(OWNERS):
        out[k] = message[k:k + 1, :]
    pl.semaphore_wait(barrier, OWNERS - 1)
    exchange(tile, rep, out, came, send_sem, recv_sem)
    arrived = jnp.concatenate([came[k] for k in range(OWNERS)], axis=0)
    pair = jnp.concatenate([arrived, pltpu.roll(arrived, 128 - 12, 1)], axis=0)
    codes[...] = pair.T


def request(rows):
    return pl.pallas_call(
        request_kernel,
        out_shape=(jax.ShapeDtypeStruct((128, 128), jnp.float32), jax.ShapeDtypeStruct((1, FIXES), jnp.float32)),
        in_specs=[VMEM] * 6,
        out_specs=(VMEM, VMEM),
        scratch_shapes=[
            pltpu.VMEM((OWNERS, 1, 128), jnp.float32),
            pltpu.VMEM((OWNERS, 1, 128), jnp.float32),
            pltpu.SemaphoreType.DMA((OWNERS,)),
            pltpu.SemaphoreType.DMA((OWNERS,)),
        ],
        compiler_params=pltpu.CompilerParams(collective_id=0, has_side_effects=True, vmem_limit_bytes=LIMIT),
    )(*rows)


def swap_rows_and_tiles(raster, turned):
    group = iota((LAYERS, 128), 1) // 16
    for half in range(2):
        for part in range(2):
            held = [raster[8 * part + t, :, half * 128:(half + 1) * 128].astype(jnp.float32) for t in range(8)]
            for step in (1, 2, 4):
                upper = (group // step) % 2 == 1
                for t in range(8):
                    if t & step == 0:
                        a, b = held[t], held[t | step]
                        held[t] = jnp.where(upper, pltpu.roll(b, 16 * step, 1), a)
                        held[t | step] = jnp.where(upper, b, pltpu.roll(a, 128 - 16 * step, 1))
            for r in range(8):
                row = 8 * half + r
                turned[row * 64:(row + 1) * 64, part * 128:(part + 1) * 128] = held[r].astype(jnp.bfloat16)


def terms_kernel(codes, raster, beta, packed, rows_out, turned, scaled, resid):
    swap_rows_and_tiles(raster, turned)
    beta_parts = stacked_thirds(beta[...])

    def block(at):
        def field(f):
            return jnp.concatenate([codes[pl.ds(f * SLOTS + 2 * at, 1), :], codes[pl.ds(f * SLOTS + 2 * at + 1, 1), :]], axis=1)

        local, anchor, frac_x, frac_y, mark = [field(f) for f in range(5)]
        row = jnp.floor((anchor + 0.5) * (1.0 / 15.0))
        cell = local * 16.0 + (anchor - 15.0 * row)
        lane = iota((256, 256), 0).astype(jnp.float32)
        weight_x = jnp.where(lane == cell, 256.0 - frac_x, 0.0) + jnp.where(lane == cell + 1.0, frac_x, 0.0)
        along = dot(turned[...], weight_x.astype(jnp.bfloat16))
        values = None
        for r in range(16):
            weight_y = jnp.where(row == float(r), 256.0 - frac_y, 0.0) + jnp.where(row == float(r - 1), frac_y, 0.0)
            term = weight_y * along[r * 64:(r + 1) * 64]
            values = term if values is None else values + term
        values = values * (1.0 / 65536.0)
        spread = jnp.broadcast_to(values[:, None, :], (LAYERS, SPLINES, 256))
        knots = 0.5 * (iota((LAYERS, SPLINES, 256), 1).astype(jnp.float32) - 0.5 * (SPLINES - 1))
        bump = jnp.maximum(1.0 - jnp.abs(spread - knots) * (1.0 / 0.75), 0.0)
        rows = (bump * bump * bump).reshape(BASIS, 256).astype(jnp.bfloat16)
        lanes = pl.ds(pl.multiple_of(at * 256, 256), 256)
        rows_out[:, lanes] = rows
        eta = jnp.sum(dot(beta_parts, rows), axis=0, keepdims=True)
        live = (mark > 0.5).astype(jnp.float32)
        outcome = mark - 1.0
        prob = 1.0 / (1.0 + jnp.exp(-eta))
        weight = prob * (1.0 - prob) * live
        scaled[:, lanes] = (jnp.sqrt(weight) * rows.astype(jnp.float32)).astype(jnp.bfloat16)
        resid[:, lanes] = stacked_thirds(weight * eta + (outcome - prob) * live)

    pl.loop(0, 6)(block)
    target = jnp.sum(dot(resid[...], rows_out[...], NT), axis=0, keepdims=True)
    for chunk in range(32):
        packed[chunk, 40:48, :] = jnp.zeros((8, 128), jnp.float32)
    for part in range(4):
        packed[part, 40:41, :] = target[:, part * 128:(part + 1) * 128]
    tile = 0
    for i in range(4):
        panel = dot(scaled[i * 128:(i + 1) * 128, :], scaled[i * 128:, :], NT)
        for j in range(i, 4):
            for r in range(16):
                packed[tile // 5, tile % 5 * 8:tile % 5 * 8 + 8, :] = panel[r * 8:r * 8 + 8, (j - i) * 128:(j - i + 1) * 128]
                tile += 1


def terms(codes, raster, beta):
    return pl.pallas_call(
        terms_kernel,
        out_shape=(
            jax.ShapeDtypeStruct((32, ROWS, 128), jnp.float32),
            jax.ShapeDtypeStruct((BASIS, OWNERS * SLOTS), jnp.bfloat16),
        ),
        in_specs=[VMEM] * 3,
        out_specs=(VMEM, VMEM),
        scratch_shapes=[
            pltpu.VMEM((1024, 256), jnp.bfloat16),
            pltpu.VMEM((BASIS, OWNERS * SLOTS), jnp.bfloat16),
            pltpu.VMEM((16, OWNERS * SLOTS), jnp.bfloat16),
        ],
        compiler_params=pltpu.CompilerParams(vmem_limit_bytes=LIMIT),
    )(codes, raster, beta)


def total_kernel(packed, out, mate_in, paired, plane_in, deep_out, deep_in, part, deep_back, whole, result,
                 s_mate, r_mate, s_plane, r_plane, s_deep, r_deep, s_back, r_back, s_wide, r_wide, s_last, r_last):
    tile, rep = position()
    x, z = lax.div(tile, DEEP), lax.rem(tile, DEEP)
    y, core = lax.div(rep, 2), lax.rem(rep, 2)
    me = x * 4 + y
    mate = (tile, rep + 1 - 2 * core)

    def chip(p):
        return (lax.div(p, 4) * DEEP + z, lax.rem(p, 4) * 2 + core)

    def level(k):
        return (x * DEEP + k, rep)

    barrier = pltpu.get_barrier_semaphore()
    pl.semaphore_signal(barrier, inc=1, device_id=mate, device_id_type=MESH)

    def greet(step, _):
        pl.semaphore_signal(barrier, inc=1, device_id=chip(lax.rem(me + step, PLANE)), device_id_type=MESH)
        pl.semaphore_signal(barrier, inc=1, device_id=level(lax.rem(z + step, DEEP)), device_id_type=MESH)
        return 0

    lax.fori_loop(1, PLANE, greet, 0)
    pl.semaphore_wait(barrier, 1 + (PLANE - 1) + (DEEP - 1))

    def remote(src, dst, send, recv, device):
        return pltpu.make_async_remote_copy(
            src_ref=src, dst_ref=dst, send_sem=send, recv_sem=recv, device_id=device, device_id_type=MESH)

    def to_mate(p):
        return remote(packed.at[(1 - core) * PLANE + p], mate_in.at[p], s_mate.at[p], r_mate.at[p], mate)

    def to_plane(p, slot):
        return remote(paired.at[p], plane_in.at[slot], s_plane.at[p], r_plane.at[slot], chip(p))

    def to_level(k, slot):
        return remote(deep_out.at[k], deep_in.at[slot], s_deep.at[k], r_deep.at[slot], level(k))

    def back_level(k, slot):
        return remote(part, deep_back.at[slot], s_back.at[k], r_back.at[slot], level(k))

    def back_plane(p, slot):
        return remote(whole, result.at[core * PLANE + slot], s_wide.at[p], r_wide.at[slot], chip(p))

    def back_mate(p, half):
        at = half * PLANE + p
        return remote(result.at[at], result.at[at], s_last.at[p], r_last.at[p], mate)

    def each(count, mine, body, first=1, last=None):
        def step(k, _):
            body(lax.rem(mine + k, count))
            return 0

        lax.fori_loop(first, count if last is None else last, step, 0)

    each(PLANE, me, lambda p: to_mate(p).start(), 1, PLANE + 1)

    def pair_sum(p):
        to_mate(p).wait_recv()
        paired[p] = packed[core * PLANE + p] + mate_in[p]

    def pair_and_send(p):
        pair_sum(p)
        to_plane(p, me).start()

    each(PLANE, me, pair_and_send)
    pair_sum(me)

    def gather_plane(k, total):
        p = lax.rem(me + k, PLANE)
        to_plane(p, p).wait_recv()
        return total + plane_in[p]

    total = lax.fori_loop(1, PLANE, gather_plane, paired[me])
    for k in range(DEEP):
        deep_out[k] = total[3 * k:3 * k + 3, :]
    each(DEEP, z, lambda k: to_level(k, z).start())

    def gather_level(step, total):
        k = lax.rem(z + step, DEEP)
        to_level(k, k).wait_recv()
        return total + deep_in[k]

    part[...] = lax.fori_loop(1, DEEP, gather_level, deep_out[z])

    each(DEEP, z, lambda k: back_level(k, z).start())
    deep_back[z] = part[...]
    each(DEEP, z, lambda k: back_level(k, k).wait_recv())
    for k in range(DEEP):
        whole[3 * k:3 * k + 3, :] = deep_back[k]
    each(PLANE, me, lambda p: back_plane(p, me).start())
    result[core * PLANE + me] = whole[...]
    back_mate(me, core).start()

    def forward(p):
        back_plane(p, p).wait_recv()
        back_mate(p, core).start()

    each(PLANE, me, forward)
    each(PLANE, me, lambda p: back_mate(p, 1 - core).wait_recv(), 0)

    each(PLANE, me, lambda p: to_mate(p).wait_send(), 0)
    each(PLANE, me, lambda p: to_plane(p, me).wait_send())
    each(DEEP, z, lambda k: to_level(k, z).wait_send())
    each(DEEP, z, lambda k: back_level(k, z).wait_send())
    each(PLANE, me, lambda p: back_plane(p, me).wait_send())
    each(PLANE, me, lambda p: back_mate(p, core).wait_send(), 0)

    def write(k, _):
        out[k] = result[k]
        return 0

    lax.fori_loop(0, 32, write, 0)


def total(packed):
    dma = pltpu.SemaphoreType.DMA((PLANE,))
    f32 = jnp.float32
    return pl.pallas_call(
        total_kernel,
        out_shape=jax.ShapeDtypeStruct((32, ROWS, 128), f32),
        in_specs=[VMEM],
        out_specs=VMEM,
        scratch_shapes=[
            pltpu.VMEM((PLANE, ROWS, 128), f32),
            pltpu.VMEM((PLANE, ROWS, 128), f32),
            pltpu.VMEM((PLANE, ROWS, 128), f32),
            pltpu.VMEM((DEEP, 3, 128), f32),
            pltpu.VMEM((DEEP, 3, 128), f32),
            pltpu.VMEM((3, 128), f32),
            pltpu.VMEM((DEEP, 3, 128), f32),
            pltpu.VMEM((ROWS, 128), f32),
            pltpu.VMEM((32, ROWS, 128), f32),
        ] + [dma] * 12,
        compiler_params=pltpu.CompilerParams(collective_id=1, has_side_effects=True, vmem_limit_bytes=LIMIT),
    )(packed)


def reciprocal(x):
    guess = pl.reciprocal(x, approx=True)
    guess = guess * (2.0 - x * guess)
    return guess * (2.0 - x * guess)


def invert(tiles):
    tiles = list(tiles)
    lane = iota((8, 128), 1)
    row = iota((8, 128), 0)

    def take(tile, m):
        return jnp.broadcast_to(tile[m:m + 1, :], (8, 128))

    for b in range(16):
        inside = (lane // 8) == b
        columns = [jnp.broadcast_to(tiles[b][:, 8 * b + m:8 * b + m + 1], (8, 128)) for m in range(8)]
        lead = jnp.where(inside, jnp.where(lane - 8 * b == row, 1.0, 0.0), tiles[b])
        for m in range(0, 8, 2):
            p, q, r = take(columns[m], m), take(columns[m + 1], m), take(columns[m + 1], m + 1)
            scale = reciprocal(p * r - q * q)
            is_first, is_second = row == m, row == m + 1

            def sweep(tile):
                first, second = take(tile, m), take(tile, m + 1)
                first, second = (r * first - q * second) * scale, (p * second - q * first) * scale
                rest = tile - columns[m] * first - columns[m + 1] * second
                return jnp.where(is_first, first, jnp.where(is_second, second, rest))

            later = [sweep(columns[k]) for k in range(m + 2, 8)]
            lead = sweep(lead)
            columns = columns[:m + 2] + later
        taken = [take(lead, m) for m in range(8)]
        for i in range(16):
            if i != b:
                source = tiles[i]
                update = jnp.where(inside, 0.0, source)
                for m in range(8):
                    update = update - jnp.broadcast_to(source[:, 8 * b + m:8 * b + m + 1], (8, 128)) * taken[m]
                tiles[i] = update
        tiles[b] = lead
    return tiles


def second_difference():
    i, j = iota((8, 128), 0), iota((8, 128), 1) % 8
    inner = jnp.zeros((8, 128), jnp.float32)

    def entry(at, r):
        return jnp.where(at == r, 1.0, 0.0) - jnp.where(at == r + 1, 2.0, 0.0) + jnp.where(at == r + 2, 1.0, 0.0)

    for r in range(SPLINES - 2):
        inner = inner + entry(i, r) * entry(j, r)
    return inner


def solve_kernel(sums, smooth, beta_new, system, scaled, right):
    count = 1.0 / (FIXES * 512.0)
    lane, row = iota((8, 128), 1), iota((8, 128), 0)
    inner = second_difference()
    tile = 0
    for i, j in BLOCKS:
        for r in range(16):
            value = sums[tile // 5, tile % 5 * 8:tile % 5 * 8 + 8, :] * count
            if i == j:
                value = value + jnp.where(lane // 8 == r, smooth[16 * i + r] * inner, 0.0)
                value = value + jnp.where(lane == row + 8 * r, RIDGE, 0.0)
            system[i, r * 8:r * 8 + 8, j * 128:(j + 1) * 128] = value
            tile += 1
    for part in range(4):
        right[part] = sums[part, 40:41, :] * count

    inverse = []
    done = []
    for k in range(4):
        tiles = invert([system[k, r * 8:r * 8 + 8, k * 128:(k + 1) * 128] for r in range(16)])
        inverse = jnp.concatenate(tiles, axis=0)
        mine = dot(jnp.broadcast_to(right[k], (8, 128)), inverse, precision=HIGHEST)
        done.append(mine)
        if k < 3:
            after = system[k, :, (k + 1) * 128:]
            spread = dot(inverse, after, precision=HIGHEST)
            scaled[k, :, (k + 1) * 128:] = spread
            shift = dot(mine, after, precision=HIGHEST)
            for i in range(k + 1, 4):
                right[i] = right[i] - shift[0:1, (i - k - 1) * 128:(i - k) * 128]
                lead = system[k, :, i * 128:(i + 1) * 128]
                change = dot(lead.T, spread[:, (i - k - 1) * 128:], precision=HIGHEST)
                system[i, :, i * 128:] = system[i, :, i * 128:] - change
    found = [None, None, None, done[3]]
    for k in (2, 1, 0):
        later = jnp.concatenate(found[k + 1:], axis=1)
        found[k] = done[k] - dot(later, scaled[k, :, (k + 1) * 128:], NT, precision=HIGHEST)
    for k in range(4):
        beta_new[:, k * 128:(k + 1) * 128] = found[k][0:1, :]


def solve(sums, smooth):
    return pl.pallas_call(
        solve_kernel,
        out_shape=jax.ShapeDtypeStruct((1, BASIS), jnp.float32),
        in_specs=[VMEM, SMEM],
        out_specs=VMEM,
        scratch_shapes=[
            pltpu.VMEM((4, 128, BASIS), jnp.float32),
            pltpu.VMEM((4, 128, BASIS), jnp.float32),
            pltpu.VMEM((4, 1, 128), jnp.float32),
        ],
        compiler_params=pltpu.CompilerParams(vmem_limit_bytes=LIMIT),
    )(sums, smooth)


def predict_rows(rows, beta_new):
    eta = jnp.sum(dot(stacked_thirds(beta_new), rows), axis=0, keepdims=True)
    lines = [eta[:, b * 128:(b + 1) * 128] for b in range(12)]
    turned = jnp.concatenate(lines + [jnp.zeros((116, 128), jnp.float32)], axis=0).T
    lane = iota((OWNERS, 128), 1)
    return jnp.where(lane < 12, turned[:OWNERS], pltpu.roll(turned[OWNERS:], 12, 1))


def unpack_rows(arrived, owner, slot):
    named = (iota((OWNERS, FIXES), 0) == owner).astype(jnp.float32).astype(jnp.bfloat16)
    high, mid, low = thirds(arrived.T)
    spread = dot(high, named) + dot(mid, named) + dot(low, named)
    at = iota((SLOTS, FIXES), 0).astype(jnp.float32) == slot
    return jnp.sum(jnp.where(at, spread[:SLOTS], 0.0), axis=0, keepdims=True)


def predict_kernel(rows, beta_new, owner, slot, eta_new, out, came, send_sem, recv_sem):
    tile, rep = position()
    barrier = pltpu.get_barrier_semaphore()
    greet_tile(barrier, tile, rep)
    message = predict_rows(rows[...], beta_new[...])
    for k in range(OWNERS):
        out[k] = message[k:k + 1, :]
    pl.semaphore_wait(barrier, OWNERS - 1)
    exchange(tile, rep, out, came, send_sem, recv_sem)
    arrived = jnp.concatenate([came[k] for k in range(OWNERS)], axis=0)
    eta_new[...] = unpack_rows(arrived, owner[...], slot[...])


def predict(rows, beta_new, owner, slot):
    return pl.pallas_call(
        predict_kernel,
        out_shape=jax.ShapeDtypeStruct((1, FIXES), jnp.float32),
        in_specs=[VMEM] * 4,
        out_specs=VMEM,
        scratch_shapes=[
            pltpu.VMEM((OWNERS, 1, 128), jnp.float32),
            pltpu.VMEM((OWNERS, 1, 128), jnp.float32),
            pltpu.SemaphoreType.DMA((OWNERS,)),
            pltpu.SemaphoreType.DMA((OWNERS,)),
        ],
        compiler_params=pltpu.CompilerParams(collective_id=2, has_side_effects=True, vmem_limit_bytes=LIMIT),
    )(rows, beta_new, owner, slot)


def shards(owner, tile_local, anchor, frac_x, frac_y, label, raster, beta, smooth):
    line = lambda array: array.reshape(1, FIXES)
    owner = line(owner)
    codes, slot = request([owner] + [line(a) for a in (tile_local, anchor, frac_x, frac_y, label)])
    packed, rows = terms(codes, raster, beta.reshape(1, BASIS))
    beta_new = solve(total(packed), smooth)
    eta_new = predict(rows, beta_new, owner, slot)
    return beta_new.reshape(BASIS), eta_new.reshape(FIXES)


def solution(mesh):
    fixes = P(("tile", "rep"))
    placed = (P(("tile", "rep"), None), fixes, fixes, fixes, fixes, fixes, P("tile", None, None), P(), P())
    return jax.shard_map(shards, mesh=mesh, in_specs=placed, out_specs=(P(), fixes), check_vma=False)
```

```python
import functools

import jax
import jax.numpy as jnp
from jax import lax
from jax.experimental import pallas as pl
from jax.experimental.pallas import tpu as pltpu
from jax.sharding import PartitionSpec as P

SPLINES = 8
RIDGE = 0.002
LAYERS = 64
BASIS = 512
FIXES = 512
SLOTS = 24
OWNERS = 64
DEEP = 16
GROUP = 32
LEVELS = 8
ROWS = 24
GRAM_TILES = 160
TARGET_ROW = GRAM_TILES % 3 * 8
MESH = pl.DeviceIdType.MESH
HIGHEST = lax.Precision.HIGHEST
VMEM = pl.BlockSpec(memory_space=pltpu.VMEM)
SMEM = pl.BlockSpec(memory_space=pltpu.SMEM)
LIMIT = 62 * 1024 * 1024
BLOCKS = [(i, j) for i in range(4) for j in range(i, 4)]
NT = (((1,), (1,)), ((), ()))
TN = (((0,), (0,)), ((), ()))


def dot(a, b, dims=(((1,), (0,)), ((), ())), precision=None):
    return lax.dot_general(a, b, dims, precision=precision, preferred_element_type=jnp.float32)


def iota(shape, axis):
    return lax.broadcasted_iota(jnp.int32, shape, axis)


def thirds(x):
    high = x.astype(jnp.bfloat16)
    rest = x - high.astype(jnp.float32)
    mid = rest.astype(jnp.bfloat16)
    low = (rest - mid.astype(jnp.float32)).astype(jnp.bfloat16)
    return high, mid, low


def stacked_thirds(x):
    high, mid, low = thirds(x)
    row = iota((16, x.shape[1]), 0)
    wide = lambda part: jnp.broadcast_to(part.astype(jnp.float32), row.shape)
    parts = jnp.where(row == 0, wide(high), jnp.where(row == 1, wide(mid), jnp.where(row == 2, wide(low), 0.0)))
    return parts.astype(jnp.bfloat16)


def position():
    return lax.axis_index("tile"), lax.axis_index("rep")


def request_rows(owner, local, anchor, frac_x, frac_y, label):
    named = (iota((OWNERS, FIXES), 0) == owner).astype(jnp.float32)
    named_b = named.astype(jnp.bfloat16)
    earlier = (iota((FIXES, FIXES), 0) < iota((FIXES, FIXES), 1)).astype(jnp.float32).astype(jnp.bfloat16)
    before = dot(named_b, earlier)
    slot = jnp.sum(before * named, axis=0, keepdims=True)
    at = iota((SLOTS, FIXES), 0).astype(jnp.float32) == slot
    fields = [field.astype(jnp.float32) for field in (local, anchor, frac_x, frac_y, label + 1)]
    spread = [jnp.where(at, field, 0.0) for field in fields] + [jnp.zeros((8, FIXES), jnp.float32)]
    spread = jnp.concatenate(spread, axis=0).astype(jnp.bfloat16)
    return dot(named_b, spread, NT), slot


def greet_tile(barrier, tile, rep):
    def greet(step, _):
        pl.semaphore_signal(barrier, inc=1, device_id=(lax.rem(tile + step, OWNERS), rep), device_id_type=MESH)
        return 0

    lax.fori_loop(1, OWNERS, greet, 0)


def exchange(tile, rep, out, came, send_sem, recv_sem):
    def copy(peer, slot):
        return pltpu.make_async_remote_copy(
            src_ref=out.at[peer], dst_ref=came.at[slot], send_sem=send_sem.at[peer], recv_sem=recv_sem.at[slot],
            device_id=(peer, rep), device_id_type=MESH)

    def begin(step, _):
        copy(lax.rem(tile + step, OWNERS), tile).start()
        return 0

    def finish(step, _):
        peer = lax.rem(tile + step, OWNERS)
        copy(peer, peer).wait_recv()
        copy(peer, peer).wait_send()
        return 0

    lax.fori_loop(1, OWNERS, begin, 0)
    came[tile] = out[tile]
    lax.fori_loop(1, OWNERS, finish, 0)


def swap_rows_and_tiles(raster, turned):
    group = iota((LAYERS, 128), 1) // 16
    for half in range(2):
        for part in range(2):
            held = [raster[8 * part + t, :, half * 128:(half + 1) * 128].astype(jnp.float32) for t in range(8)]
            for step in (1, 2, 4):
                upper = (group // step) % 2 == 1
                for t in range(8):
                    if t & step == 0:
                        a, b = held[t], held[t | step]
                        held[t] = jnp.where(upper, pltpu.roll(b, 16 * step, 1), a)
                        held[t | step] = jnp.where(upper, b, pltpu.roll(a, 128 - 16 * step, 1))
            for r in range(8):
                row = 8 * half + r
                turned[row * 64:(row + 1) * 64, part * 128:(part + 1) * 128] = held[r].astype(jnp.bfloat16)


def form_terms(codes, beta, packed, rows_out, turned, scaled, resid):
    beta_parts = stacked_thirds(beta[...])

    def block(at):
        def field(f):
            return jnp.concatenate([codes[pl.ds(f * SLOTS + 2 * at, 1), :], codes[pl.ds(f * SLOTS + 2 * at + 1, 1), :]], axis=1)

        local, anchor, frac_x, frac_y, mark = [field(f) for f in range(5)]
        row = jnp.floor((anchor + 0.5) * (1.0 / 15.0))
        cell = local * 16.0 + (anchor - 15.0 * row)
        lane = iota((256, 256), 0).astype(jnp.float32)
        weight_x = jnp.where(lane == cell, 256.0 - frac_x, 0.0) + jnp.where(lane == cell + 1.0, frac_x, 0.0)
        along = dot(turned[...], weight_x.astype(jnp.bfloat16))
        values = None
        for r in range(16):
            weight_y = jnp.where(row == float(r), 256.0 - frac_y, 0.0) + jnp.where(row == float(r - 1), frac_y, 0.0)
            term = weight_y * along[r * 64:(r + 1) * 64]
            values = term if values is None else values + term
        values = values * (1.0 / 65536.0)
        spread = jnp.broadcast_to(values[:, None, :], (LAYERS, SPLINES, 256))
        knots = 0.5 * (iota((LAYERS, SPLINES, 256), 1).astype(jnp.float32) - 0.5 * (SPLINES - 1))
        bump = jnp.maximum(1.0 - jnp.abs(spread - knots) * (1.0 / 0.75), 0.0)
        rows = (bump * bump * bump).reshape(BASIS, 256).astype(jnp.bfloat16)
        lanes = pl.ds(pl.multiple_of(at * 256, 256), 256)
        rows_out[:, lanes] = rows
        eta = jnp.sum(dot(beta_parts, rows), axis=0, keepdims=True)
        live = (mark > 0.5).astype(jnp.float32)
        outcome = mark - 1.0
        prob = 1.0 / (1.0 + jnp.exp(-eta))
        weight = prob * (1.0 - prob) * live
        scaled[:, lanes] = (jnp.sqrt(weight) * rows.astype(jnp.float32)).astype(jnp.bfloat16)
        resid[:, lanes] = stacked_thirds(weight * eta + (outcome - prob) * live)

    pl.loop(0, 6)(block)
    target = jnp.sum(dot(resid[...], rows_out[...], NT), axis=0, keepdims=True)
    for spare in range(GRAM_TILES, 2 * GROUP * 3):
        packed[spare // 3, spare % 3 * 8:spare % 3 * 8 + 8, :] = jnp.zeros((8, 128), jnp.float32)
    for part in range(4):
        packed[GRAM_TILES // 3, TARGET_ROW + part:TARGET_ROW + part + 1, :] = target[:, part * 128:(part + 1) * 128]
    tile = 0
    for i in range(4):
        panel = dot(scaled[i * 128:(i + 1) * 128, :], scaled[i * 128:, :], NT)
        for j in range(i, 4):
            for r in range(16):
                packed[tile // 3, tile % 3 * 8:tile % 3 * 8 + 8, :] = panel[r * 8:r * 8 + 8, (j - i) * 128:(j - i + 1) * 128]
                tile += 1


def add_up(place, packed, mate_in, paired, group_in, mine, level_in, whole, result, sems):
    s_mate, r_mate, s_group, r_group, s_level, r_level, s_wide, r_wide, s_last, r_last = sems
    me, core, pair, mate, chip, level = place

    def remote(src, dst, send, recv, device):
        return pltpu.make_async_remote_copy(
            src_ref=src, dst_ref=dst, send_sem=send, recv_sem=recv, device_id=device, device_id_type=MESH)

    def to_mate(p):
        return remote(packed.at[(1 - core) * GROUP + p], mate_in.at[p], s_mate.at[p], r_mate.at[p], mate)

    def to_chip(p, slot):
        return remote(paired.at[p], group_in.at[slot], s_group.at[p], r_group.at[slot], chip(p))

    def to_level(k, slot):
        return remote(mine, level_in.at[slot], s_level.at[k], r_level.at[slot], level(k))

    def back_chip(p, slot):
        return remote(whole, result.at[core * GROUP + slot], s_wide.at[p], r_wide.at[slot], chip(p))

    def back_mate(p, half):
        at = half * GROUP + p
        return remote(result.at[at], result.at[at], s_last.at[p], r_last.at[p], mate)

    def each(body, first=1, last=GROUP):
        def step(k, _):
            body(lax.rem(me + k, GROUP))
            return 0

        lax.fori_loop(first, last, step, 0)

    each(lambda p: to_mate(p).start(), 1, GROUP + 1)

    def pair_sum(p):
        to_mate(p).wait_recv()
        paired[p] = packed[core * GROUP + p] + mate_in[p]

    def pair_and_send(p):
        pair_sum(p)
        to_chip(p, me).start()

    each(pair_and_send)
    pair_sum(me)

    def gather(k, total):
        p = lax.rem(me + k, GROUP)
        to_chip(p, p).wait_recv()
        return total + group_in[p]

    mine[...] = lax.fori_loop(1, GROUP, gather, paired[me])
    others = [lax.rem(pair + step, LEVELS) for step in (4, 3, 5, 2, 6, 1, 7)]
    for k in others:
        to_level(k, pair).start()
    level_in[pair] = mine[...]
    for k in others:
        to_level(k, k).wait_recv()
    total = level_in[0]
    for k in range(1, LEVELS):
        total = total + level_in[k]
    whole[...] = total

    each(lambda p: back_chip(p, me).start())
    result[core * GROUP + me] = total
    back_mate(me, core).start()

    def forward(p):
        back_chip(p, p).wait_recv()
        back_mate(p, core).start()

    each(forward)
    each(lambda p: back_mate(p, 1 - core).wait_recv(), 0)

    each(lambda p: to_mate(p).wait_send(), 0)
    each(lambda p: to_chip(p, me).wait_send())
    for k in others:
        to_level(k, pair).wait_send()
    each(lambda p: back_chip(p, me).wait_send())
    each(lambda p: back_mate(p, core).wait_send(), 0)


def sums_kernel(owner, local, anchor, frac_x, frac_y, label, raster, beta, out, rows_out, slot_out,
                lines, raster_in, beta_in, out_codes, came, codes, turned, scaled, resid,
                packed, mate_in, paired, group_in, mine, level_in, whole, result, loads, send_sem, recv_sem, *sems):
    tile, rep = position()
    x, z = lax.div(tile, DEEP), lax.rem(tile, DEEP)
    y, core = lax.div(rep, 2), lax.rem(rep, 2)
    pair, low = lax.div(z, 2), lax.rem(z, 2)
    me = (x * 4 + y) * 2 + low
    mate = (tile, rep + 1 - 2 * core)

    def chip(p):
        return (lax.div(p, 8) * DEEP + pair * 2 + lax.rem(p, 2), lax.rem(lax.div(p, 2), 4) * 2 + core)

    def level(k):
        return (x * DEEP + k * 2 + low, rep)

    barrier = pltpu.get_barrier_semaphore()
    greet_tile(barrier, tile, rep)
    pl.semaphore_signal(barrier, inc=1, device_id=mate, device_id_type=MESH)

    def greet(step, _):
        other_y = lax.rem(y + 1 + lax.rem(step, 3), 4)
        rest = lax.div(step, 3)
        device = (lax.div(rest, 2) * DEEP + pair * 2 + lax.rem(rest, 2), other_y * 2 + core)
        pl.semaphore_signal(barrier, inc=1, device_id=device, device_id_type=MESH)
        return 0

    lax.fori_loop(0, 24, greet, 0)

    arguments = [(source, lines.at[k]) for k, source in enumerate((owner, local, anchor, frac_x, frac_y, label))]
    arguments += [(raster, raster_in), (beta, beta_in)]
    copies = [pltpu.make_async_copy(source, target, loads.at[k]) for k, (source, target) in enumerate(arguments)]
    for copy in copies:
        copy.start()
    for copy in copies[:6]:
        copy.wait()
    message, slot = request_rows(*[lines[k] for k in range(6)])
    slot_out[...] = slot
    for k in range(OWNERS):
        out_codes[k] = message[k:k + 1, :]
    copies[6].wait()
    copies[7].wait()
    swap_rows_and_tiles(raster_in, turned)
    pl.semaphore_wait(barrier, OWNERS - 1 + 24 + 1)
    exchange(tile, rep, out_codes, came, send_sem, recv_sem)
    arrived = jnp.concatenate([came[k] for k in range(OWNERS)], axis=0)
    codes[...] = jnp.concatenate([arrived, pltpu.roll(arrived, 128 - 12, 1)], axis=0).T
    form_terms(codes, beta_in, packed, rows_out, turned, scaled, resid)
    add_up((me, core, pair, mate, chip, level), packed, mate_in, paired, group_in, mine, level_in, whole, result, sems)

    def write(k, _):
        out[k] = result[k]
        return 0

    lax.fori_loop(0, 2 * GROUP, write, 0)


def sums(lines, raster, beta):
    f32, bf16, i32 = jnp.float32, jnp.bfloat16, jnp.int32
    group = pltpu.SemaphoreType.DMA((GROUP,))
    deep = pltpu.SemaphoreType.DMA((LEVELS,))
    tiles = pltpu.SemaphoreType.DMA((OWNERS,))
    return pl.pallas_call(
        sums_kernel,
        out_shape=(
            jax.ShapeDtypeStruct((2 * GROUP, ROWS, 128), f32),
            jax.ShapeDtypeStruct((BASIS, OWNERS * SLOTS), bf16),
            jax.ShapeDtypeStruct((1, FIXES), f32),
        ),
        in_specs=[pl.BlockSpec(memory_space=pltpu.HBM)] * 8,
        out_specs=(VMEM, VMEM, VMEM),
        scratch_shapes=[
            pltpu.VMEM((6, 1, FIXES), i32),
            pltpu.VMEM((16, LAYERS, 256), bf16),
            pltpu.VMEM((1, BASIS), f32),
            pltpu.VMEM((OWNERS, 1, 128), f32),
            pltpu.VMEM((OWNERS, 1, 128), f32),
            pltpu.VMEM((128, 128), f32),
            pltpu.VMEM((1024, 256), bf16),
            pltpu.VMEM((BASIS, OWNERS * SLOTS), bf16),
            pltpu.VMEM((16, OWNERS * SLOTS), bf16),
            pltpu.VMEM((2 * GROUP, ROWS, 128), f32),
            pltpu.VMEM((GROUP, ROWS, 128), f32),
            pltpu.VMEM((GROUP, ROWS, 128), f32),
            pltpu.VMEM((GROUP, ROWS, 128), f32),
            pltpu.VMEM((ROWS, 128), f32),
            pltpu.VMEM((LEVELS, ROWS, 128), f32),
            pltpu.VMEM((ROWS, 128), f32),
            pltpu.VMEM((2 * GROUP, ROWS, 128), f32),
            pltpu.SemaphoreType.DMA((8,)),
            tiles, tiles, group, group, group, group, deep, deep, group, group, group, group,
        ],
        compiler_params=pltpu.CompilerParams(collective_id=0, has_side_effects=True, vmem_limit_bytes=LIMIT),
    )(*lines, raster, beta)


def reciprocal(x):
    guess = pl.reciprocal(x, approx=True)
    guess = guess * (2.0 - x * guess)
    return guess * (2.0 - x * guess)


def invert(tiles):
    tiles = list(tiles)
    lane = iota((8, 128), 1)
    row = iota((8, 128), 0)

    def take(tile, m):
        return jnp.broadcast_to(tile[m:m + 1, :], (8, 128))

    for b in range(16):
        inside = (lane // 8) == b
        columns = [jnp.broadcast_to(tiles[b][:, 8 * b + m:8 * b + m + 1], (8, 128)) for m in range(8)]
        lead = jnp.where(inside, jnp.where(lane - 8 * b == row, 1.0, 0.0), tiles[b])
        for m in range(0, 8, 2):
            p, q, r = take(columns[m], m), take(columns[m + 1], m), take(columns[m + 1], m + 1)
            scale = reciprocal(p * r - q * q)
            is_first, is_second = row == m, row == m + 1

            def sweep(tile):
                first, second = take(tile, m), take(tile, m + 1)
                first, second = (r * first - q * second) * scale, (p * second - q * first) * scale
                rest = tile - columns[m] * first - columns[m + 1] * second
                return jnp.where(is_first, first, jnp.where(is_second, second, rest))

            later = [sweep(columns[k]) for k in range(m + 2, 8)]
            lead = sweep(lead)
            columns = columns[:m + 2] + later
        taken = [take(lead, m) for m in range(8)]
        for i in range(16):
            if i != b:
                source = tiles[i]
                update = jnp.where(inside, 0.0, source)
                for m in range(8):
                    update = update - jnp.broadcast_to(source[:, 8 * b + m:8 * b + m + 1], (8, 128)) * taken[m]
                tiles[i] = update
        tiles[b] = lead
    return tiles


def second_difference():
    i, j = iota((8, 128), 0), iota((8, 128), 1) % 8
    inner = jnp.zeros((8, 128), jnp.float32)

    def entry(at, r):
        return jnp.where(at == r, 1.0, 0.0) - jnp.where(at == r + 1, 2.0, 0.0) + jnp.where(at == r + 2, 1.0, 0.0)

    for r in range(SPLINES - 2):
        inner = inner + entry(i, r) * entry(j, r)
    return inner


def solve_system(sums, smooth, beta_new, system, scaled, right):
    count = 1.0 / (FIXES * 512.0)
    lane, row = iota((8, 128), 1), iota((8, 128), 0)
    inner = second_difference()
    tile = 0
    for i, j in BLOCKS:
        for r in range(16):
            value = sums[tile // 3, tile % 3 * 8:tile % 3 * 8 + 8, :] * count
            if i == j:
                value = value + jnp.where(lane // 8 == r, smooth[16 * i + r] * inner, 0.0)
                value = value + jnp.where(lane == row + 8 * r, RIDGE, 0.0)
            system[i, r * 8:r * 8 + 8, j * 128:(j + 1) * 128] = value
            tile += 1
    for part in range(4):
        right[part] = sums[GRAM_TILES // 3, TARGET_ROW + part:TARGET_ROW + part + 1, :] * count

    inverse = []
    done = []
    for k in range(4):
        tiles = invert([system[k, r * 8:r * 8 + 8, k * 128:(k + 1) * 128] for r in range(16)])
        inverse = jnp.concatenate(tiles, axis=0)
        mine = dot(jnp.broadcast_to(right[k], (8, 128)), inverse, precision=HIGHEST)
        done.append(mine)
        if k < 3:
            after = system[k, :, (k + 1) * 128:]
            spread = dot(inverse, after, precision=HIGHEST)
            scaled[k, :, (k + 1) * 128:] = spread
            shift = dot(mine, after, precision=HIGHEST)
            for i in range(k + 1, 4):
                right[i] = right[i] - shift[0:1, (i - k - 1) * 128:(i - k) * 128]
                lead = system[k, :, i * 128:(i + 1) * 128]
                change = dot(lead.T, spread[:, (i - k - 1) * 128:], precision=HIGHEST)
                system[i, :, i * 128:] = system[i, :, i * 128:] - change
    found = [None, None, None, done[3]]
    for k in (2, 1, 0):
        later = jnp.concatenate(found[k + 1:], axis=1)
        found[k] = done[k] - dot(later, scaled[k, :, (k + 1) * 128:], NT, precision=HIGHEST)
    for k in range(4):
        beta_new[:, k * 128:(k + 1) * 128] = found[k][0:1, :]


def predict_rows(rows, beta_new):
    eta = jnp.sum(dot(stacked_thirds(beta_new), rows), axis=0, keepdims=True)
    lines = [eta[:, b * 128:(b + 1) * 128] for b in range(12)]
    turned = jnp.concatenate(lines + [jnp.zeros((116, 128), jnp.float32)], axis=0).T
    lane = iota((OWNERS, 128), 1)
    return jnp.where(lane < 12, turned[:OWNERS], pltpu.roll(turned[OWNERS:], 12, 1))


def unpack_rows(arrived, owner, slot):
    named = (iota((OWNERS, FIXES), 0) == owner).astype(jnp.float32).astype(jnp.bfloat16)
    high, mid, low = thirds(arrived.T)
    spread = dot(high, named) + dot(mid, named) + dot(low, named)
    at = iota((SLOTS, FIXES), 0).astype(jnp.float32) == slot
    return jnp.sum(jnp.where(at, spread[:SLOTS], 0.0), axis=0, keepdims=True)


def finish_kernel(sums, smooth, rows, owner, slot, beta_new, eta_new, system, scaled, right, out, came, send_sem, recv_sem):
    tile, rep = position()
    barrier = pltpu.get_barrier_semaphore()
    greet_tile(barrier, tile, rep)
    solve_system(sums, smooth, beta_new, system, scaled, right)
    message = predict_rows(rows[...], beta_new[...])
    for k in range(OWNERS):
        out[k] = message[k:k + 1, :]
    pl.semaphore_wait(barrier, OWNERS - 1)
    exchange(tile, rep, out, came, send_sem, recv_sem)
    arrived = jnp.concatenate([came[k] for k in range(OWNERS)], axis=0)
    eta_new[...] = unpack_rows(arrived, owner[...], slot[...])


def finish(sums, smooth, rows, owner, slot):
    f32 = jnp.float32
    tiles = pltpu.SemaphoreType.DMA((OWNERS,))
    return pl.pallas_call(
        finish_kernel,
        out_shape=(jax.ShapeDtypeStruct((1, BASIS), f32), jax.ShapeDtypeStruct((1, FIXES), f32)),
        in_specs=[VMEM, SMEM, VMEM, VMEM, VMEM],
        out_specs=(VMEM, VMEM),
        scratch_shapes=[
            pltpu.VMEM((4, 128, BASIS), f32),
            pltpu.VMEM((4, 128, BASIS), f32),
            pltpu.VMEM((4, 1, 128), f32),
            pltpu.VMEM((OWNERS, 1, 128), f32),
            pltpu.VMEM((OWNERS, 1, 128), f32),
            tiles, tiles,
        ],
        compiler_params=pltpu.CompilerParams(collective_id=1, has_side_effects=True, vmem_limit_bytes=LIMIT),
    )(sums, smooth, rows, owner, slot)


def shards(owner, tile_local, anchor, frac_x, frac_y, label, raster, beta, smooth):
    lines = [array.reshape(1, FIXES) for array in (owner, tile_local, anchor, frac_x, frac_y, label)]
    added, rows, slot = sums(lines, raster, beta.reshape(1, BASIS))
    beta_new, eta_new = finish(added, smooth, rows, lines[0], slot)
    return beta_new.reshape(BASIS), eta_new.reshape(FIXES)


def solution(mesh):
    fixes = P(("tile", "rep"))
    placed = (P(("tile", "rep"), None), fixes, fixes, fixes, fixes, fixes, P("tile", None, None), P(), P())
    return jax.shard_map(shards, mesh=mesh, in_specs=placed, out_specs=(P(), fixes), check_vma=False)
```

```python
import functools

import jax
import jax.numpy as jnp
from jax import lax
from jax.experimental import pallas as pl
from jax.experimental.pallas import tpu as pltpu
from jax.sharding import PartitionSpec as P

SPLINES = 8
RIDGE = 0.002
LAYERS = 64
BASIS = 512
FIXES = 512
SLOTS = 24
OWNERS = 64
DEEP = 16
GROUP = 32
LEVELS = 8
ROWS = 24
GRAM_TILES = 160
TARGET_ROW = GRAM_TILES % 3 * 8
REACH = 2.5
STEPS = 13104.0
MESH = pl.DeviceIdType.MESH
HIGHEST = lax.Precision.HIGHEST
VMEM = pl.BlockSpec(memory_space=pltpu.VMEM)
SMEM = pl.BlockSpec(memory_space=pltpu.SMEM)
LIMIT = 62 * 1024 * 1024
BLOCKS = [(i, j) for i in range(4) for j in range(i, 4)]
NT = (((1,), (1,)), ((), ()))
TN = (((0,), (0,)), ((), ()))


def dot(a, b, dims=(((1,), (0,)), ((), ())), precision=None):
    return lax.dot_general(a, b, dims, precision=precision, preferred_element_type=jnp.float32)


def iota(shape, axis):
    return lax.broadcasted_iota(jnp.int32, shape, axis)


def thirds(x):
    high = x.astype(jnp.bfloat16)
    rest = x - high.astype(jnp.float32)
    mid = rest.astype(jnp.bfloat16)
    low = (rest - mid.astype(jnp.float32)).astype(jnp.bfloat16)
    return high, mid, low


def stacked_thirds(x):
    high, mid, low = thirds(x)
    row = iota((16, x.shape[1]), 0)
    wide = lambda part: jnp.broadcast_to(part.astype(jnp.float32), row.shape)
    parts = jnp.where(row == 0, wide(high), jnp.where(row == 1, wide(mid), jnp.where(row == 2, wide(low), 0.0)))
    return parts.astype(jnp.bfloat16)


def remote(src, dst, send, recv, device):
    return pltpu.make_async_remote_copy(
        src_ref=src, dst_ref=dst, send_sem=send, recv_sem=recv, device_id=device, device_id_type=MESH)


def position():
    return lax.axis_index("tile"), lax.axis_index("rep")


def request_rows(owner, local, anchor, frac_x, frac_y, label):
    named = (iota((OWNERS, FIXES), 0) == owner).astype(jnp.float32)
    named_b = named.astype(jnp.bfloat16)
    earlier = (iota((FIXES, FIXES), 0) < iota((FIXES, FIXES), 1)).astype(jnp.float32).astype(jnp.bfloat16)
    before = dot(named_b, earlier)
    slot = jnp.sum(before * named, axis=0, keepdims=True)
    at = iota((SLOTS, FIXES), 0).astype(jnp.float32) == slot
    fields = [field.astype(jnp.float32) for field in (local, anchor, frac_x, frac_y, label + 1)]
    spread = [jnp.where(at, field, 0.0) for field in fields] + [jnp.zeros((8, FIXES), jnp.float32)]
    spread = jnp.concatenate(spread, axis=0).astype(jnp.bfloat16)
    return dot(named_b, spread, NT), slot


def greet_tile(barrier, tile, rep):
    def greet(step, _):
        pl.semaphore_signal(barrier, inc=1, device_id=(lax.rem(tile + step, OWNERS), rep), device_id_type=MESH)
        return 0

    lax.fori_loop(1, OWNERS, greet, 0)


def send_all(tile, rep, out, came, send_sem, recv_sem):
    def begin(step, _):
        peer = lax.rem(tile + step, OWNERS)
        remote(out.at[peer], came.at[tile], send_sem, recv_sem, (peer, rep)).start()
        return 0

    lax.fori_loop(1, OWNERS, begin, 0)
    came[tile] = out[tile]


def all_messages(tile, rep, out, came, send_sem, recv_sem):
    many = pl.ds(0, OWNERS - 1)
    return remote(out.at[many], came.at[many], send_sem, recv_sem, (lax.rem(tile + 1, OWNERS), rep))


def swap_rows_and_tiles(raster, turned):
    group = iota((LAYERS, 128), 1) // 16
    for half in range(2):
        for part in range(2):
            held = [raster[8 * part + t, :, half * 128:(half + 1) * 128].astype(jnp.float32) for t in range(8)]
            for step in (1, 2, 4):
                upper = (group // step) % 2 == 1
                for t in range(8):
                    if t & step == 0:
                        a, b = held[t], held[t | step]
                        held[t] = jnp.where(upper, pltpu.roll(b, 16 * step, 1), a)
                        held[t | step] = jnp.where(upper, b, pltpu.roll(a, 128 - 16 * step, 1))
            for r in range(8):
                row = 8 * half + r
                turned[row * 64:(row + 1) * 64, part * 128:(part + 1) * 128] = held[r].astype(jnp.bfloat16)


def expand(values):
    shape = (LAYERS, SPLINES, values.shape[1])
    spread = jnp.broadcast_to(values[:, None, :], shape)
    knots = 0.5 * (iota(shape, 1).astype(jnp.float32) - 0.5 * (SPLINES - 1))
    bump = jnp.maximum(1.0 - jnp.abs(spread - knots) * (1.0 / 0.75), 0.0)
    return (bump * bump * bump).reshape(BASIS, values.shape[1]).astype(jnp.bfloat16)


def form_terms(codes, beta, packed, coded, rows_out, turned, scaled, resid):
    beta_parts = stacked_thirds(beta[...])

    def block(at):
        def field(f):
            return jnp.concatenate([codes[pl.ds(f * SLOTS + 2 * at, 1), :], codes[pl.ds(f * SLOTS + 2 * at + 1, 1), :]], axis=1)

        local, anchor, frac_x, frac_y, mark = [field(f) for f in range(5)]
        row = jnp.floor((anchor + 0.5) * (1.0 / 15.0))
        cell = local * 16.0 + (anchor - 15.0 * row)
        lane = iota((256, 256), 0).astype(jnp.float32)
        weight_x = jnp.where(lane == cell, 256.0 - frac_x, 0.0) + jnp.where(lane == cell + 1.0, frac_x, 0.0)
        along = dot(turned[...], weight_x.astype(jnp.bfloat16))
        values = None
        for r in range(16):
            weight_y = jnp.where(row == float(r), 256.0 - frac_y, 0.0) + jnp.where(row == float(r - 1), frac_y, 0.0)
            term = weight_y * along[r * 64:(r + 1) * 64]
            values = term if values is None else values + term
        values = values * (1.0 / 65536.0)
        lanes = pl.ds(pl.multiple_of(at * 256, 256), 256)
        coded[:, lanes] = jnp.floor(jnp.clip(values, -REACH, REACH) * STEPS + 0.5).astype(jnp.int32)
        rows = expand(values)
        rows_out[:, lanes] = rows
        eta = jnp.sum(dot(beta_parts, rows), axis=0, keepdims=True)
        live = (mark > 0.5).astype(jnp.float32)
        outcome = mark - 1.0
        prob = 1.0 / (1.0 + jnp.exp(-eta))
        weight = prob * (1.0 - prob) * live
        scaled[:, lanes] = (jnp.sqrt(weight) * rows.astype(jnp.float32)).astype(jnp.bfloat16)
        resid[:, lanes] = stacked_thirds(weight * eta + (outcome - prob) * live)

    pl.loop(0, 6)(block)
    target = jnp.sum(dot(resid[...], rows_out[...], NT), axis=0, keepdims=True)
    for spare in range(GRAM_TILES, 2 * GROUP * 3):
        packed[spare // 3, spare % 3 * 8:spare % 3 * 8 + 8, :] = jnp.zeros((8, 128), jnp.float32)
    for part in range(4):
        packed[GRAM_TILES // 3, TARGET_ROW + part:TARGET_ROW + part + 1, :] = target[:, part * 128:(part + 1) * 128]
    tile = 0
    for i in range(4):
        panel = dot(scaled[i * 128:(i + 1) * 128, :], scaled[i * 128:, :], NT)
        for j in range(i, 4):
            for r in range(16):
                packed[tile // 3, tile % 3 * 8:tile % 3 * 8 + 8, :] = panel[r * 8:r * 8 + 8, (j - i) * 128:(j - i + 1) * 128]
                tile += 1


def add_up(place, packed, mate_in, paired, group_in, mine, level_in, whole, result, sems, while_down, while_back):
    s_mate, r_mate, s_group, r_group, s_level, r_level, s_wide, r_wide, s_last, r_last = sems
    me, core, pair, mate, chip, level = place
    peer = chip(lax.rem(me + 1, GROUP))
    most = pl.ds(0, GROUP - 1)

    def to_mate(p):
        return remote(packed.at[(1 - core) * GROUP + p], mate_in.at[p], s_mate, r_mate.at[p], mate)

    def back_chip(p, slot):
        return remote(whole, result.at[core * GROUP + slot], s_wide.at[p], r_wide.at[slot], chip(p))

    def back_mate(p):
        at = core * GROUP + p
        return remote(result.at[at], result.at[at], s_last, r_last, mate)

    def each(body, first=1, last=GROUP):
        def step(k, _):
            body(lax.rem(me + k, GROUP))
            return 0

        lax.fori_loop(first, last, step, 0)

    each(lambda p: to_mate(p).start(), 1, GROUP + 1)

    def pair_sum(p):
        to_mate(p).wait_recv()
        paired[p] = packed[core * GROUP + p] + mate_in[p]

    def pair_and_send(p):
        pair_sum(p)
        remote(paired.at[p], group_in.at[me], s_group, r_group, chip(p)).start()

    each(pair_and_send)
    pair_sum(me)
    group_in[me] = paired[me]
    while_down()
    all_group = remote(paired.at[most], group_in.at[most], s_group, r_group, peer)
    all_group.wait_recv()

    def gather(k, total):
        return total + (group_in[4 * k] + group_in[4 * k + 1]) + (group_in[4 * k + 2] + group_in[4 * k + 3])

    mine[...] = lax.fori_loop(0, GROUP // 4, gather, jnp.zeros((ROWS, 128), jnp.float32))
    others = [lax.rem(pair + step, LEVELS) for step in (4, 3, 5, 2, 6, 1, 7)]
    for k in others:
        remote(mine, level_in.at[pair], s_level.at[k], r_level.at[pair], level(k)).start()
    level_in[pair] = mine[...]
    for k in others:
        remote(mine, level_in.at[k], s_level.at[k], r_level.at[k], level(k)).wait_recv()
    total = level_in[0]
    for k in range(1, LEVELS):
        total = total + level_in[k]
    whole[...] = total

    each(lambda p: back_chip(p, me).start())
    result[core * GROUP + me] = total
    back_mate(me).start()
    while_back()

    def forward(p):
        back_chip(p, p).wait_recv()
        back_mate(p).start()

    each(forward)
    theirs = result.at[pl.ds((1 - core) * GROUP, GROUP)]
    remote(theirs, theirs, s_last, r_last, mate).wait_recv()

    def settle():
        remote(mate_in, mate_in, s_mate, s_mate, mate).wait_send()
        all_group.wait_send()
        for k in others:
            remote(mine, level_in.at[k], s_level.at[k], r_level.at[k], level(k)).wait_send()
        each(lambda p: back_chip(p, me).wait_send())
        remote(theirs, theirs, s_last, r_last, mate).wait_send()

    return settle


def pack_values(coded, out):
    for t in range(3):
        words = []
        for r in (2 * t, 2 * t + 1):
            low, high = coded[:, r * 128:(r + 1) * 128], coded[:, (r + 6) * 128:(r + 7) * 128]
            words.append((low & 65535) | (high << 16))
        turned = jnp.concatenate(words, axis=0).T
        for k in range(OWNERS):
            out[k, 2 * t:2 * t + 1, :] = turned[k:k + 1, :]
            out[k, 2 * t + 1:2 * t + 2, :] = turned[OWNERS + k:OWNERS + k + 1, :]


def unpack_words(came, bytes_out, t):
    words = jnp.concatenate([came[k, 2 * t + half:2 * t + half + 1, :] for half in range(2) for k in range(OWNERS)], axis=0).T
    for which, codes in enumerate(((words << 16) >> 16, words >> 16)):
        for r in range(2):
            code = codes[r * 64:(r + 1) * 64, :]
            upper, lower = code >> 8, code & 255
            both = jnp.concatenate([upper, lower], axis=0).astype(jnp.float32).astype(jnp.bfloat16)
            block = 6 * which + 2 * t + r
            bytes_out[:, block * 128:(block + 1) * 128] = both


def values_of_fixes(bytes_in, owner, slot):
    second = slot >= 12.0
    key = jnp.where(second, (slot - 12.0) * 128.0 + 64.0, slot * 128.0) + owner.astype(jnp.float32)
    place = iota((OWNERS * SLOTS, key.shape[1]), 0).astype(jnp.float32)
    picked = dot(bytes_in[...], (place == key).astype(jnp.float32).astype(jnp.bfloat16))
    return (picked[:LAYERS] * 256.0 + picked[LAYERS:]) * (1.0 / STEPS)


def reciprocal(x):
    guess = pltpu.reciprocal(x, approx=True)
    return guess * (2.0 - x * guess)


def add_tree(terms):
    while len(terms) > 1:
        terms = [terms[k] + terms[k + 1] if k + 1 < len(terms) else terms[k] for k in range(0, len(terms), 2)]
    return terms[0]


def six_left(x):
    high, mid, low = thirds(x)
    return jnp.concatenate([high, high, high, mid, mid, low], axis=1)


def six_right(x):
    high, mid, low = thirds(x)
    return jnp.concatenate([high, mid, low, high, mid, high], axis=0)


def invert(tiles, chores):
    tiles, chores = list(tiles), list(chores)
    share = -(-len(chores) // 15)
    lane = iota((8, 128), 1)
    row = iota((8, 128), 0)

    def take(tile, m):
        return jnp.broadcast_to(tile[m:m + 1, :], (8, 128))

    def column(tile, at):
        return jnp.broadcast_to(tile[:, at:at + 1], (8, 128))

    for b in range(16):
        inside = (lane // 8) == b
        columns = [column(tiles[b], 8 * b + m) for m in range(8)]
        lead = jnp.where(inside, jnp.where(lane - 8 * b == row, 1.0, 0.0), tiles[b])
        for m in range(0, 8, 2):
            p, q, r = take(columns[m], m), take(columns[m + 1], m), take(columns[m + 1], m + 1)
            scale = reciprocal(p * r - q * q)
            is_first, is_second = row == m, row == m + 1

            def sweep(tile):
                first, second = take(tile, m), take(tile, m + 1)
                first, second = r * first - q * second, p * second - q * first
                rest = tile - (columns[m] * first + columns[m + 1] * second) * scale
                return jnp.where(is_first, first * scale, jnp.where(is_second, second * scale, rest))

            later = [sweep(columns[k]) for k in range(m + 2, 8)]
            lead = sweep(lead)
            columns = columns[:m + 2] + later
        taken = [take(lead, m) for m in range(8)]
        order = [(b + 1 + s) % 16 for s in range(15)]
        far = order[8:]
        left = jnp.concatenate([jnp.where(inside, tiles[i], 0.0) for i in far], axis=0)
        blank = lambda n: [jnp.zeros((8 * n, 128), jnp.float32)] if n else []
        change = dot(six_left(left), six_right(jnp.concatenate(blank(b) + [lead] + blank(15 - b), axis=0)))
        for i in order[:8]:
            terms = [column(tiles[i], 8 * b + m) * taken[m] for m in range(8)]
            tiles[i] = jnp.where(inside, 0.0, tiles[i]) - add_tree(terms)
        for s, i in enumerate(far):
            tiles[i] = jnp.where(inside, 0.0, tiles[i]) - change[8 * s:8 * s + 8, :]
        tiles[b] = lead
        for chore in chores[b * share:(b + 1) * share]:
            chore()
    return tiles


def second_difference():
    i, j = iota((8, 128), 0), iota((8, 128), 1) % 8
    inner = jnp.zeros((8, 128), jnp.float32)

    def entry(at, r):
        return jnp.where(at == r, 1.0, 0.0) - jnp.where(at == r + 1, 2.0, 0.0) + jnp.where(at == r + 2, 1.0, 0.0)

    for r in range(SPLINES - 2):
        inner = inner + entry(i, r) * entry(j, r)
    return inner


def solve_system(sums, smooth, beta_new, system, spread, late_chores):
    count = 1.0 / (FIXES * 512.0)
    lane, row = iota((8, 128), 1), iota((8, 128), 0)
    inner = second_difference()
    tile = 0
    for i, j in BLOCKS:
        for r in range(16):
            value = sums[tile // 3, tile % 3 * 8:tile % 3 * 8 + 8, :] * count
            if i == j:
                value = value + jnp.where(lane // 8 == r, smooth[16 * i + r] * inner, 0.0)
                value = value + jnp.where(lane == row + 8 * r, RIDGE, 0.0)
            system[i, r * 8:r * 8 + 8, j * 128:(j + 1) * 128] = value
            tile += 1
    for part in range(4):
        line = sums[GRAM_TILES // 3, TARGET_ROW + part:TARGET_ROW + part + 1, :] * count
        system[part, :, 512:640] = jnp.broadcast_to(line, (128, 128)).T

    def spread_of(k, inverse, start, stop):
        part = dot(inverse, six_right(system[k, :, start:stop]))
        system[k, :, start:stop] = part
        spread[:, start:stop] = six_right(part)

    def eliminate(i, left, start, stop):
        system[i, :, start:stop] = system[i, :, start:stop] - dot(left, spread[:, start:stop])

    pending = []
    for k in range(4):
        diagonal = [system[k, r * 8:r * 8 + 8, k * 128:(k + 1) * 128] for r in range(16)]
        inverse = six_left(jnp.concatenate(invert(diagonal, pending), axis=0))
        near = (k + 1) * 128
        lefts = {i: six_left(system[k, :, i * 128:(i + 1) * 128].T) for i in range(k + 1, 4)}
        lefts.update({i: six_left(system[i, :, k * 128:(k + 1) * 128]) for i in range(k)})
        spread_of(k, inverse, near, near + 128)
        pending = []
        if k < 3:
            eliminate(k + 1, lefts[k + 1], near, near + 128)
            pending.append(functools.partial(spread_of, k, inverse, near + 128, 640))
            pending.append(functools.partial(eliminate, k + 1, lefts[k + 1], near + 128, 640))
            for i in range(k + 2, 4):
                pending.append(functools.partial(eliminate, i, lefts[i], i * 128, 640))
            for i in range(k):
                pending.append(functools.partial(eliminate, i, lefts[i], near, 640))
        else:
            for i in range(k):
                eliminate(i, lefts[i], 512, 640)
        if k == 2:
            pending += late_chores
    for k in range(4):
        beta_new[:, k * 128:(k + 1) * 128] = system[k, :, 512:640].T[0:1, :]


def step_kernel(owner, local, anchor, frac_x, frac_y, label, raster, beta, smooth, beta_new, eta_new,
                lines, raster_in, beta_in, out_codes, came, codes, turned, rows, scaled, resid, coded,
                packed, mate_in, paired, group_in, mine, level_in, whole, result,
                out_values, came_values, value_bytes, own_rows, slot_row, system, spread,
                loads, send_codes, recv_codes, send_values, recv_values, *sems):
    tile, rep = position()
    x, z = lax.div(tile, DEEP), lax.rem(tile, DEEP)
    y, core = lax.div(rep, 2), lax.rem(rep, 2)
    pair, low = lax.div(z, 2), lax.rem(z, 2)
    me = (x * 4 + y) * 2 + low
    mate = (tile, rep + 1 - 2 * core)

    def chip(p):
        return (lax.div(p, 8) * DEEP + pair * 2 + lax.rem(p, 2), lax.rem(lax.div(p, 2), 4) * 2 + core)

    def level(k):
        return (x * DEEP + k * 2 + low, rep)

    barrier = pltpu.get_barrier_semaphore()
    greet_tile(barrier, tile, rep)
    pl.semaphore_signal(barrier, inc=1, device_id=mate, device_id_type=MESH)

    def greet(step, _):
        other_y = lax.rem(y + 1 + lax.rem(step, 3), 4)
        rest = lax.div(step, 3)
        device = (lax.div(rest, 2) * DEEP + pair * 2 + lax.rem(rest, 2), other_y * 2 + core)
        pl.semaphore_signal(barrier, inc=1, device_id=device, device_id_type=MESH)
        return 0

    lax.fori_loop(0, 24, greet, 0)

    arguments = [(source, lines.at[k]) for k, source in enumerate((owner, local, anchor, frac_x, frac_y, label))]
    arguments += [(raster, raster_in), (beta, beta_in)]
    copies = [pltpu.make_async_copy(source, target, loads.at[k]) for k, (source, target) in enumerate(arguments)]
    for copy in copies:
        copy.start()
    for copy in copies[:6]:
        copy.wait()
    message, slot = request_rows(*[lines[k] for k in range(6)])
    slot_row[...] = slot
    for k in range(OWNERS):
        out_codes[k] = message[k:k + 1, :]
    copies[6].wait()
    copies[7].wait()
    swap_rows_and_tiles(raster_in, turned)
    pl.semaphore_wait(barrier, OWNERS - 1 + 24 + 1)

    codes_sent = (tile, rep, out_codes, came, send_codes, recv_codes)
    send_all(*codes_sent)
    all_messages(*codes_sent).wait_recv()
    arrived = jnp.concatenate([came[k] for k in range(OWNERS)], axis=0)
    codes[...] = jnp.concatenate([arrived, pltpu.roll(arrived, 128 - 12, 1)], axis=0).T
    form_terms(codes, beta_in, packed, coded, rows, turned, scaled, resid)

    values_sent = (tile, rep, out_values, came_values, send_values, recv_values)
    settle = add_up(
        (me, core, pair, mate, chip, level), packed, mate_in, paired, group_in, mine, level_in, whole, result, sems,
        lambda: pack_values(coded, out_values), lambda: send_all(*values_sent))

    def place_rows(part):
        values = values_of_fixes(value_bytes, lines[0, :, part * 128:(part + 1) * 128], slot_row[:, part * 128:(part + 1) * 128])
        own_rows[:, part * 128:(part + 1) * 128] = expand(values)

    chores = [settle, lambda: all_messages(*codes_sent).wait_send(), lambda: all_messages(*values_sent).wait_recv()]
    chores += [functools.partial(unpack_words, came_values, value_bytes, t) for t in range(3)]
    chores += [functools.partial(place_rows, part) for part in range(4)]
    solve_system(result, smooth, beta_new, system, spread, chores)
    eta_new[...] = jnp.sum(dot(stacked_thirds(beta_new[...]), own_rows[...]), axis=0, keepdims=True)
    all_messages(*values_sent).wait_send()


def step(lines, raster, beta, smooth):
    f32, bf16, i32 = jnp.float32, jnp.bfloat16, jnp.int32
    one = pltpu.SemaphoreType.DMA
    group = pltpu.SemaphoreType.DMA((GROUP,))
    deep = pltpu.SemaphoreType.DMA((LEVELS,))
    chunks = pltpu.VMEM((GROUP, ROWS, 128), f32)
    chunk = pltpu.VMEM((ROWS, 128), f32)
    served = OWNERS * SLOTS
    return pl.pallas_call(
        step_kernel,
        out_shape=(jax.ShapeDtypeStruct((1, BASIS), f32), jax.ShapeDtypeStruct((1, FIXES), f32)),
        in_specs=[pl.BlockSpec(memory_space=pltpu.HBM)] * 8 + [SMEM],
        out_specs=(VMEM, VMEM),
        scratch_shapes=[
            pltpu.VMEM((6, 1, FIXES), i32),
            pltpu.VMEM((16, LAYERS, 256), bf16),
            pltpu.VMEM((1, BASIS), f32),
            pltpu.VMEM((OWNERS, 1, 128), f32),
            pltpu.VMEM((OWNERS, 1, 128), f32),
            pltpu.VMEM((128, 128), f32),
            pltpu.VMEM((1024, 256), bf16),
            pltpu.VMEM((BASIS, served), bf16),
            pltpu.VMEM((BASIS, served), bf16),
            pltpu.VMEM((16, served), bf16),
            pltpu.VMEM((LAYERS, served), i32),
            pltpu.VMEM((2 * GROUP, ROWS, 128), f32),
            chunks, chunks, chunks,
            chunk,
            pltpu.VMEM((LEVELS, ROWS, 128), f32),
            chunk,
            pltpu.VMEM((2 * GROUP, ROWS, 128), f32),
            pltpu.VMEM((OWNERS, 6, 128), i32),
            pltpu.VMEM((OWNERS, 6, 128), i32),
            pltpu.VMEM((128, served), bf16),
            pltpu.VMEM((BASIS, FIXES), bf16),
            pltpu.VMEM((1, FIXES), f32),
            pltpu.VMEM((4, 128, BASIS + 128), f32),
            pltpu.VMEM((768, BASIS + 128), bf16),
            pltpu.SemaphoreType.DMA((8,)),
            one, one, one, one,
            one, group, one, one, deep, deep, group, group, one, one,
        ],
        compiler_params=pltpu.CompilerParams(collective_id=0, has_side_effects=True, vmem_limit_bytes=LIMIT),
    )(*lines, raster, beta, smooth)


def shards(owner, tile_local, anchor, frac_x, frac_y, label, raster, beta, smooth):
    lines = [array.reshape(1, FIXES) for array in (owner, tile_local, anchor, frac_x, frac_y, label)]
    beta_new, eta_new = step(lines, raster, beta.reshape(1, BASIS), smooth)
    return beta_new.reshape(BASIS), eta_new.reshape(FIXES)


def solution(mesh):
    fixes = P(("tile", "rep"))
    placed = (P(("tile", "rep"), None), fixes, fixes, fixes, fixes, fixes, P("tile", None, None), P(), P())
    return jax.shard_map(shards, mesh=mesh, in_specs=placed, out_specs=(P(), fixes), check_vma=False)
```

```python
import functools

import jax
import jax.numpy as jnp
from jax import lax
from jax.experimental import pallas as pl
from jax.experimental.pallas import tpu as pltpu
from jax.sharding import PartitionSpec as P

SPLINES = 8
RIDGE = 0.002
LAYERS = 64
BASIS = 512
FIXES = 512
SLOTS = 24
OWNERS = 64
DEEP = 16
GROUP = 32
LEVELS = 8
ROWS = 24
GRAM_TILES = 160
TARGET_ROW = GRAM_TILES % 3 * 8
FIRST = 3
REACH = 2.5
STEPS = 13104.0
MESH = pl.DeviceIdType.MESH
HIGHEST = lax.Precision.HIGHEST
VMEM = pl.BlockSpec(memory_space=pltpu.VMEM)
SMEM = pl.BlockSpec(memory_space=pltpu.SMEM)
LIMIT = 62 * 1024 * 1024
BLOCKS = [(i, j) for i in range(4) for j in range(i, 4)]
NT = (((1,), (1,)), ((), ()))
TN = (((0,), (0,)), ((), ()))


def dot(a, b, dims=(((1,), (0,)), ((), ())), precision=None):
    return lax.dot_general(a, b, dims, precision=precision, preferred_element_type=jnp.float32)


def iota(shape, axis):
    return lax.broadcasted_iota(jnp.int32, shape, axis)


def thirds(x):
    high = x.astype(jnp.bfloat16)
    rest = x - high.astype(jnp.float32)
    mid = rest.astype(jnp.bfloat16)
    low = (rest - mid.astype(jnp.float32)).astype(jnp.bfloat16)
    return high, mid, low


def add_tree(terms):
    while len(terms) > 1:
        terms = [terms[k] + terms[k + 1] if k + 1 < len(terms) else terms[k] for k in range(0, len(terms), 2)]
    return terms[0]


def stacked_thirds(x):
    high, mid, low = thirds(x)
    row = iota((16, x.shape[1]), 0)
    wide = lambda part: jnp.broadcast_to(part.astype(jnp.float32), row.shape)
    parts = jnp.where(row == 0, wide(high), jnp.where(row == 1, wide(mid), jnp.where(row == 2, wide(low), 0.0)))
    return parts.astype(jnp.bfloat16)


def remote(src, dst, send, recv, device):
    return pltpu.make_async_remote_copy(
        src_ref=src, dst_ref=dst, send_sem=send, recv_sem=recv, device_id=device, device_id_type=MESH)


def position():
    return lax.axis_index("tile"), lax.axis_index("rep")


def request_rows(owner, local, anchor, frac_x, frac_y, label):
    named = (iota((OWNERS, FIXES), 0) == owner).astype(jnp.float32)
    named_b = named.astype(jnp.bfloat16)
    earlier = (iota((FIXES, FIXES), 0) < iota((FIXES, FIXES), 1)).astype(jnp.float32).astype(jnp.bfloat16)
    before = dot(named_b, earlier)
    slot = jnp.sum(before * named, axis=0, keepdims=True)
    at = iota((SLOTS, FIXES), 0).astype(jnp.float32) == slot
    fields = [field.astype(jnp.float32) for field in (local, anchor, frac_x, frac_y, label + 1)]
    spread = [jnp.where(at, field, 0.0) for field in fields] + [jnp.zeros((8, FIXES), jnp.float32)]
    spread = jnp.concatenate(spread, axis=0).astype(jnp.bfloat16)
    return dot(named_b, spread, NT), slot


def other_owners(tile):
    x, z = lax.div(tile, DEEP), lax.rem(tile, DEEP)
    reach = lambda step, size: min(step, size - step)
    steps = [(dx, dz) for dx in range(4) for dz in range(DEEP) if dx or dz]
    for dx, dz in sorted(steps, key=lambda step: -(reach(step[0], 4) + reach(step[1], DEEP))):
        yield lax.rem(x + dx, 4) * DEEP + lax.rem(z + dz, DEEP)


def greet_tile(barrier, tile, rep):
    for peer in other_owners(tile):
        pl.semaphore_signal(barrier, inc=1, device_id=(peer, rep), device_id_type=MESH)


def send_some(peers, tile, rep, out, came, send_sem, recv_sem):
    for peer in peers:
        remote(out.at[peer], came.at[tile], send_sem, recv_sem, (peer, rep)).start()


def all_messages(tile, rep, out, came, send_sem, recv_sem):
    many = pl.ds(0, OWNERS - 1)
    return remote(out.at[many], came.at[many], send_sem, recv_sem, (lax.rem(tile + 1, OWNERS), rep))


def swap_rows_and_tiles(raster, turned):
    group = iota((LAYERS, 128), 1) // 16
    for half in range(2):
        for part in range(2):
            held = [raster[8 * part + t, :, half * 128:(half + 1) * 128].astype(jnp.float32) for t in range(8)]
            for step in (1, 2, 4):
                upper = (group // step) % 2 == 1
                for t in range(8):
                    if t & step == 0:
                        a, b = held[t], held[t | step]
                        held[t] = jnp.where(upper, pltpu.roll(b, 16 * step, 1), a)
                        held[t | step] = jnp.where(upper, b, pltpu.roll(a, 128 - 16 * step, 1))
            for r in range(8):
                row = 8 * half + r
                turned[row * 64:(row + 1) * 64, part * 128:(part + 1) * 128] = held[r].astype(jnp.bfloat16)


def expand(values):
    shape = (LAYERS, SPLINES, values.shape[1])
    spread = jnp.broadcast_to(values[:, None, :], shape)
    knots = 0.5 * (iota(shape, 1).astype(jnp.float32) - 0.5 * (SPLINES - 1))
    bump = jnp.maximum(1.0 - jnp.abs(spread - knots) * (1.0 / 0.75), 0.0)
    return (bump * bump * bump).reshape(BASIS, values.shape[1]).astype(jnp.bfloat16)


def form_terms(codes, beta, packed, coded, rows_out, turned, scaled, resid, panel_done):
    beta_parts = stacked_thirds(beta[...])

    def block(at):
        def field(f):
            return jnp.concatenate([codes[pl.ds(f * SLOTS + 2 * at, 1), :], codes[pl.ds(f * SLOTS + 2 * at + 1, 1), :]], axis=1)

        local, anchor, frac_x, frac_y, mark = [field(f) for f in range(5)]
        row = jnp.floor((anchor + 0.5) * (1.0 / 15.0))
        cell = local * 16.0 + (anchor - 15.0 * row)
        lane = iota((256, 256), 0).astype(jnp.float32)
        weight_x = jnp.where(lane == cell, 256.0 - frac_x, 0.0) + jnp.where(lane == cell + 1.0, frac_x, 0.0)
        along = dot(turned[...], weight_x.astype(jnp.bfloat16))
        values = None
        for r in range(16):
            weight_y = jnp.where(row == float(r), 256.0 - frac_y, 0.0) + jnp.where(row == float(r - 1), frac_y, 0.0)
            term = weight_y * along[r * 64:(r + 1) * 64]
            values = term if values is None else values + term
        values = values * (1.0 / 65536.0)
        lanes = pl.ds(pl.multiple_of(at * 256, 256), 256)
        coded[:, lanes] = jnp.floor(jnp.clip(values, -REACH, REACH) * STEPS + 0.5).astype(jnp.int32)
        rows = expand(values)
        rows_out[:, lanes] = rows
        eta = jnp.sum(dot(beta_parts, rows), axis=0, keepdims=True)
        live = (mark > 0.5).astype(jnp.float32)
        outcome = mark - 1.0
        prob = 1.0 / (1.0 + jnp.exp(-eta))
        weight = prob * (1.0 - prob) * live
        scaled[:, lanes] = (jnp.sqrt(weight) * rows.astype(jnp.float32)).astype(jnp.bfloat16)
        resid[:, lanes] = stacked_thirds(weight * eta + (outcome - prob) * live)

    pl.loop(0, 6)(block)
    target = jnp.sum(dot(resid[...], rows_out[...], NT), axis=0, keepdims=True)
    for spare in range(GRAM_TILES, 2 * GROUP * 3):
        packed[spare // 3, spare % 3 * 8:spare % 3 * 8 + 8, :] = jnp.zeros((8, 128), jnp.float32)
    for part in range(4):
        packed[GRAM_TILES // 3, TARGET_ROW + part:TARGET_ROW + part + 1, :] = target[:, part * 128:(part + 1) * 128]
    tile = 0
    for i in range(4):
        panel = dot(scaled[i * 128:(i + 1) * 128, :], scaled[i * 128:, :], NT)
        for j in range(i, 4):
            for r in range(16):
                packed[tile // 3, tile % 3 * 8:tile % 3 * 8 + 8, :] = panel[r * 8:r * 8 + 8, (j - i) * 128:(j - i + 1) * 128]
                tile += 1
        panel_done(tile // 6 if i < 3 else GROUP)


def add_up(place, packed, mate_in, paired, group_in, mine, level_in, whole, result, sems, while_down):
    s_mate, r_mate, s_group, r_group, s_level, r_level, s_wide, r_wide, s_last, r_last = sems
    me, core, pair, mate, chip, level = place
    peer = chip(lax.rem(me + 1, GROUP))
    most = pl.ds(0, GROUP - 1)
    others = [lax.rem(pair + step, LEVELS) for step in (4, 3, 5, 2, 6, 1, 7)]
    around = [lax.rem(me + step, GROUP) for step in range(1, GROUP)]
    sent = [0]

    def to_mate(p):
        return remote(packed.at[2 * p + 1 - core], mate_in.at[p], s_mate, r_mate.at[p], mate)

    def back_chip(p, slot):
        return remote(whole, result.at[2 * slot + core], s_wide, r_wide.at[slot], chip(p))

    def back_mate(p, whose):
        chunk = result.at[2 * p + whose]
        return remote(chunk, chunk, s_last, r_last.at[p], mate)

    def all_group():
        return remote(paired.at[most], group_in.at[most], s_group, r_group, peer)

    def send_ready(stop):
        for p in range(sent[0], stop):
            to_mate(p).start()
        sent[0] = stop

    def pair_sum(p):
        to_mate(p).wait_recv()
        paired[p] = packed[2 * p + core] + mate_in[p]

    def forward(p):
        @pl.when(p != me)
        def _():
            back_chip(p, p).wait_recv()
            back_mate(p, core).start()

    def down_and_first(first):
        for p in around:
            pair_sum(p)
            remote(paired.at[p], group_in.at[me], s_group, r_group, chip(p)).start()
        pair_sum(me)
        group_in[me] = paired[me]
        while_down()
        all_group().wait_recv()
        mine[...] = add_tree([group_in[p] for p in range(GROUP)])
        for k in others:
            remote(mine, level_in.at[pair], s_level.at[k], r_level.at[pair], level(k)).start()
        level_in[pair] = mine[...]
        for k in others:
            remote(mine, level_in.at[k], s_level.at[k], r_level.at[k], level(k)).wait_recv()
        total = add_tree([level_in[k] for k in range(LEVELS)])
        whole[...] = total
        result[2 * me + core] = total
        for p in around:
            back_chip(p, me).start()
        back_mate(me, core).start()
        for p in range(first):
            forward(p)
        for p in range(first):
            back_mate(p, 1 - core).wait_recv()

    def forward_rest(start, stop):
        def one(p, _):
            forward(p)
            return 0

        lax.fori_loop(start, stop, one, 0)

    def wait_rest(start):
        def one(p, _):
            back_mate(p, 1 - core).wait_recv()
            return 0

        lax.fori_loop(start, GROUP, one, 0)

    def settle():
        remote(mate_in, mate_in, s_mate, s_mate, mate).wait_send()
        all_group().wait_send()
        for k in others:
            remote(mine, level_in.at[k], s_level.at[k], r_level.at[k], level(k)).wait_send()
        some = result.at[most]
        remote(some, some, s_wide, s_wide, peer).wait_send()
        half = result.at[pl.ds(0, GROUP)]
        remote(half, half, s_last, s_last, mate).wait_send()

    return send_ready, down_and_first, forward_rest, wait_rest, settle


def pack_values(coded, out):
    for t in range(3):
        words = []
        for r in (2 * t, 2 * t + 1):
            low, high = coded[:, r * 128:(r + 1) * 128], coded[:, (r + 6) * 128:(r + 7) * 128]
            words.append((low & 65535) | (high << 16))
        turned = jnp.concatenate(words, axis=0).T
        for k in range(OWNERS):
            out[k, 2 * t:2 * t + 1, :] = turned[k:k + 1, :]
            out[k, 2 * t + 1:2 * t + 2, :] = turned[OWNERS + k:OWNERS + k + 1, :]


def unpack_words(came, bytes_out, t):
    words = jnp.concatenate([came[k, 2 * t + half:2 * t + half + 1, :] for half in range(2) for k in range(OWNERS)], axis=0).T
    for which, codes in enumerate(((words << 16) >> 16, words >> 16)):
        for r in range(2):
            code = codes[r * 64:(r + 1) * 64, :]
            upper, lower = code >> 8, code & 255
            both = jnp.concatenate([upper, lower], axis=0).astype(jnp.float32).astype(jnp.bfloat16)
            block = 6 * which + 2 * t + r
            bytes_out[:, block * 128:(block + 1) * 128] = both


def values_of_fixes(bytes_in, owner, slot):
    second = slot >= 12.0
    key = jnp.where(second, (slot - 12.0) * 128.0 + 64.0, slot * 128.0) + owner.astype(jnp.float32)
    place = iota((OWNERS * SLOTS, key.shape[1]), 0).astype(jnp.float32)
    picked = dot(bytes_in[...], (place == key).astype(jnp.float32).astype(jnp.bfloat16))
    return (picked[:LAYERS] * 256.0 + picked[LAYERS:]) * (1.0 / STEPS)


def reciprocal(x):
    guess = pltpu.reciprocal(x, approx=True)
    return guess * (2.0 - x * guess)


def six_left(x):
    high, mid, low = thirds(x)
    return jnp.concatenate([high, high, high, mid, mid, low], axis=1)


def six_right(x):
    high, mid, low = thirds(x)
    return jnp.concatenate([high, mid, low, high, mid, high], axis=0)


def invert(tiles, chores):
    tiles, chores = list(tiles), list(chores)
    share = -(-len(chores) // 15)
    lane = iota((8, 128), 1)
    row = iota((8, 128), 0)

    def take(tile, m):
        return jnp.broadcast_to(tile[m:m + 1, :], (8, 128))

    def column(tile, at):
        return jnp.broadcast_to(tile[:, at:at + 1], (8, 128))

    for b in range(16):
        inside = (lane // 8) == b
        columns = [column(tiles[b], 8 * b + m) for m in range(8)]
        lead = jnp.where(inside, jnp.where(lane - 8 * b == row, 1.0, 0.0), tiles[b])
        for m in range(0, 8, 2):
            p, q, r = take(columns[m], m), take(columns[m + 1], m), take(columns[m + 1], m + 1)
            scale = reciprocal(p * r - q * q)
            is_first, is_second = row == m, row == m + 1

            def sweep(tile):
                first, second = take(tile, m), take(tile, m + 1)
                first, second = r * first - q * second, p * second - q * first
                rest = tile - (columns[m] * first + columns[m + 1] * second) * scale
                return jnp.where(is_first, first * scale, jnp.where(is_second, second * scale, rest))

            later = [sweep(columns[k]) for k in range(m + 2, 8)]
            lead = sweep(lead)
            columns = columns[:m + 2] + later
        taken = [take(lead, m) for m in range(8)]
        order = [(b + 1 + s) % 16 for s in range(15)]
        far = order[8:]
        left = jnp.concatenate([jnp.where(inside, tiles[i], 0.0) for i in far], axis=0)
        blank = lambda n: [jnp.zeros((8 * n, 128), jnp.float32)] if n else []
        change = dot(six_left(left), six_right(jnp.concatenate(blank(b) + [lead] + blank(15 - b), axis=0)))
        for i in order[:8]:
            terms = [column(tiles[i], 8 * b + m) * taken[m] for m in range(8)]
            tiles[i] = jnp.where(inside, 0.0, tiles[i]) - add_tree(terms)
        for s, i in enumerate(far):
            tiles[i] = jnp.where(inside, 0.0, tiles[i]) - change[8 * s:8 * s + 8, :]
        tiles[b] = lead
        for chore in chores[b * share:(b + 1) * share]:
            chore()
    return tiles


def second_difference():
    i, j = iota((8, 128), 0), iota((8, 128), 1) % 8
    inner = jnp.zeros((8, 128), jnp.float32)

    def entry(at, r):
        return jnp.where(at == r, 1.0, 0.0) - jnp.where(at == r + 1, 2.0, 0.0) + jnp.where(at == r + 2, 1.0, 0.0)

    for r in range(SPLINES - 2):
        inner = inner + entry(i, r) * entry(j, r)
    return inner


def solve_system(sums, smooth, beta_new, system, spread, first_chores, late_chores):
    count = 1.0 / (FIXES * 512.0)
    lane, row = iota((8, 128), 1), iota((8, 128), 0)
    inner = second_difference()

    def assemble(number):
        i, j = BLOCKS[number]
        for r in range(16):
            tile = 16 * number + r
            value = sums[tile // 3, tile % 3 * 8:tile % 3 * 8 + 8, :] * count
            if i == j:
                value = value + jnp.where(lane // 8 == r, smooth[16 * i + r] * inner, 0.0)
                value = value + jnp.where(lane == row + 8 * r, RIDGE, 0.0)
            system[i, r * 8:r * 8 + 8, j * 128:(j + 1) * 128] = value

    def assemble_right():
        for part in range(4):
            line = sums[GRAM_TILES // 3, TARGET_ROW + part:TARGET_ROW + part + 1, :] * count
            system[part, :, 512:640] = jnp.broadcast_to(line, (128, 128)).T

    assemble(0)
    def spread_of(k, inverse, start, stop):
        part = dot(inverse, six_right(system[k, :, start:stop]))
        system[k, :, start:stop] = part
        spread[:, start:stop] = six_right(part)

    def eliminate(i, left, start, stop):
        system[i, :, start:stop] = system[i, :, start:stop] - dot(left, spread[:, start:stop])

    pending = first_chores + [functools.partial(assemble, number) for number in range(1, 10)] + [assemble_right]
    for k in range(4):
        diagonal = [system[k, r * 8:r * 8 + 8, k * 128:(k + 1) * 128] for r in range(16)]
        inverse = six_left(jnp.concatenate(invert(diagonal, pending), axis=0))
        near = (k + 1) * 128
        lefts = {i: six_left(system[k, :, i * 128:(i + 1) * 128].T) for i in range(k + 1, 4)}
        lefts.update({i: six_left(system[i, :, k * 128:(k + 1) * 128]) for i in range(k)})
        spread_of(k, inverse, near, near + 128)
        pending = []
        if k < 3:
            eliminate(k + 1, lefts[k + 1], near, near + 128)
            pending.append(functools.partial(spread_of, k, inverse, near + 128, 640))
            pending.append(functools.partial(eliminate, k + 1, lefts[k + 1], near + 128, 640))
            for i in range(k + 2, 4):
                pending.append(functools.partial(eliminate, i, lefts[i], i * 128, 640))
            for i in range(k):
                pending.append(functools.partial(eliminate, i, lefts[i], near, 640))
        else:
            for i in range(k):
                eliminate(i, lefts[i], 512, 640)
        if k == 2:
            pending += late_chores
    for k in range(4):
        beta_new[:, k * 128:(k + 1) * 128] = system[k, :, 512:640].T[0:1, :]


def step_kernel(owner, local, anchor, frac_x, frac_y, label, raster, beta, smooth, beta_new, eta_new,
                lines, raster_in, beta_in, out_codes, came, codes, turned, rows, scaled, resid, coded,
                packed, mate_in, paired, group_in, mine, level_in, whole, result,
                out_values, came_values, value_bytes, own_rows, slot_row, system, spread,
                loads, send_codes, recv_codes, send_values, recv_values, *sems):
    tile, rep = position()
    x, z = lax.div(tile, DEEP), lax.rem(tile, DEEP)
    y, core = lax.div(rep, 2), lax.rem(rep, 2)
    pair, low = lax.div(z, 2), lax.rem(z, 2)
    me = (x * 4 + y) * 2 + low
    mate = (tile, rep + 1 - 2 * core)

    def chip(p):
        return (lax.div(p, 8) * DEEP + pair * 2 + lax.rem(p, 2), lax.rem(lax.div(p, 2), 4) * 2 + core)

    def level(k):
        return (x * DEEP + k * 2 + low, rep)

    barrier = pltpu.get_barrier_semaphore()
    greet_tile(barrier, tile, rep)
    pl.semaphore_signal(barrier, inc=1, device_id=mate, device_id_type=MESH)

    def greet(step, _):
        other_y = lax.rem(y + 1 + lax.rem(step, 3), 4)
        rest = lax.div(step, 3)
        device = (lax.div(rest, 2) * DEEP + pair * 2 + lax.rem(rest, 2), other_y * 2 + core)
        pl.semaphore_signal(barrier, inc=1, device_id=device, device_id_type=MESH)
        return 0

    lax.fori_loop(0, 24, greet, 0)

    arguments = [(source, lines.at[k]) for k, source in enumerate((owner, local, anchor, frac_x, frac_y, label))]
    arguments += [(raster, raster_in), (beta, beta_in)]
    copies = [pltpu.make_async_copy(source, target, loads.at[k]) for k, (source, target) in enumerate(arguments)]
    for copy in copies:
        copy.start()
    for copy in copies[:6]:
        copy.wait()
    message, slot = request_rows(*[lines[k] for k in range(6)])
    slot_row[...] = slot
    for k in range(OWNERS):
        out_codes[k] = message[k:k + 1, :]
    copies[6].wait()
    copies[7].wait()
    swap_rows_and_tiles(raster_in, turned)
    pl.semaphore_wait(barrier, OWNERS - 1 + 24 + 1)

    codes_sent = (tile, rep, out_codes, came, send_codes, recv_codes)
    came[tile] = out_codes[tile]
    send_some(other_owners(tile), *codes_sent)
    all_messages(*codes_sent).wait_recv()
    arrived = jnp.concatenate([came[k] for k in range(OWNERS)], axis=0)
    codes[...] = jnp.concatenate([arrived, pltpu.roll(arrived, 128 - 12, 1)], axis=0).T
    values_sent = (tile, rep, out_values, came_values, send_values, recv_values)
    send_ready, down_and_first, forward_rest, wait_rest, settle = add_up(
        (me, core, pair, mate, chip, level), packed, mate_in, paired, group_in, mine, level_in, whole, result, sems,
        lambda: pack_values(coded, out_values))
    form_terms(codes, beta_in, packed, coded, rows, turned, scaled, resid, send_ready)
    down_and_first(FIRST)

    def place_rows(part):
        values = values_of_fixes(value_bytes, lines[0, :, part * 128:(part + 1) * 128], slot_row[:, part * 128:(part + 1) * 128])
        own_rows[:, part * 128:(part + 1) * 128] = expand(values)

    peers = list(other_owners(tile))
    half = (FIRST + GROUP) // 2
    first_chores = [functools.partial(forward_rest, FIRST, half), functools.partial(forward_rest, half, GROUP)]
    first_chores += [functools.partial(send_some, peers[k:k + 21], *values_sent) for k in range(0, OWNERS - 1, 21)]
    first_chores += [functools.partial(wait_rest, FIRST)]

    def settle_all():
        settle()
        all_messages(*codes_sent).wait_send()
        came_values[tile] = out_values[tile]
        all_messages(*values_sent).wait_recv()

    chores = [settle_all]
    chores += [functools.partial(unpack_words, came_values, value_bytes, t) for t in range(3)]
    chores += [functools.partial(place_rows, part) for part in range(4)]
    solve_system(result, smooth, beta_new, system, spread, first_chores, chores)
    eta_new[...] = jnp.sum(dot(stacked_thirds(beta_new[...]), own_rows[...]), axis=0, keepdims=True)
    all_messages(*values_sent).wait_send()


def step(lines, raster, beta, smooth):
    f32, bf16, i32 = jnp.float32, jnp.bfloat16, jnp.int32
    one = pltpu.SemaphoreType.DMA
    group = pltpu.SemaphoreType.DMA((GROUP,))
    deep = pltpu.SemaphoreType.DMA((LEVELS,))
    chunks = pltpu.VMEM((GROUP, ROWS, 128), f32)
    chunk = pltpu.VMEM((ROWS, 128), f32)
    served = OWNERS * SLOTS
    return pl.pallas_call(
        step_kernel,
        out_shape=(jax.ShapeDtypeStruct((1, BASIS), f32), jax.ShapeDtypeStruct((1, FIXES), f32)),
        in_specs=[pl.BlockSpec(memory_space=pltpu.HBM)] * 8 + [SMEM],
        out_specs=(VMEM, VMEM),
        scratch_shapes=[
            pltpu.VMEM((6, 1, FIXES), i32),
            pltpu.VMEM((16, LAYERS, 256), bf16),
            pltpu.VMEM((1, BASIS), f32),
            pltpu.VMEM((OWNERS, 1, 128), f32),
            pltpu.VMEM((OWNERS, 1, 128), f32),
            pltpu.VMEM((128, 128), f32),
            pltpu.VMEM((1024, 256), bf16),
            pltpu.VMEM((BASIS, served), bf16),
            pltpu.VMEM((BASIS, served), bf16),
            pltpu.VMEM((16, served), bf16),
            pltpu.VMEM((LAYERS, served), i32),
            pltpu.VMEM((2 * GROUP, ROWS, 128), f32),
            chunks, chunks, chunks,
            chunk,
            pltpu.VMEM((LEVELS, ROWS, 128), f32),
            chunk,
            pltpu.VMEM((2 * GROUP, ROWS, 128), f32),
            pltpu.VMEM((OWNERS, 6, 128), i32),
            pltpu.VMEM((OWNERS, 6, 128), i32),
            pltpu.VMEM((128, served), bf16),
            pltpu.VMEM((BASIS, FIXES), bf16),
            pltpu.VMEM((1, FIXES), f32),
            pltpu.VMEM((4, 128, BASIS + 128), f32),
            pltpu.VMEM((768, BASIS + 128), bf16),
            pltpu.SemaphoreType.DMA((8,)),
            one, one, one, one,
            one, group, one, one, deep, deep, one, group, one, group,
        ],
        compiler_params=pltpu.CompilerParams(collective_id=0, has_side_effects=True, vmem_limit_bytes=LIMIT),
    )(*lines, raster, beta, smooth)


def shards(owner, tile_local, anchor, frac_x, frac_y, label, raster, beta, smooth):
    lines = [array.reshape(1, FIXES) for array in (owner, tile_local, anchor, frac_x, frac_y, label)]
    beta_new, eta_new = step(lines, raster, beta.reshape(1, BASIS), smooth)
    return beta_new.reshape(BASIS), eta_new.reshape(FIXES)


def solution(mesh):
    fixes = P(("tile", "rep"))
    placed = (P(("tile", "rep"), None), fixes, fixes, fixes, fixes, fixes, P("tile", None, None), P(), P())
    return jax.shard_map(shards, mesh=mesh, in_specs=placed, out_specs=(P(), fixes), check_vma=False)
```

```python
import functools

import jax
import jax.numpy as jnp
from jax import lax
from jax.experimental import pallas as pl
from jax.experimental.pallas import tpu as pltpu
from jax.sharding import PartitionSpec as P

SPLINES = 8
RIDGE = 0.002
LAYERS = 64
BASIS = 512
FIXES = 512
SLOTS = 24
OWNERS = 64
DEEP = 16
GROUP = 32
LEVELS = 8
ROWS = 24
GRAM_TILES = 160
TARGET_ROW = GRAM_TILES % 3 * 8
USED = 27
FIRST = 3
REACH = 2.5
STEPS = 13104.0
MESH = pl.DeviceIdType.MESH
HIGHEST = lax.Precision.HIGHEST
VMEM = pl.BlockSpec(memory_space=pltpu.VMEM)
SMEM = pl.BlockSpec(memory_space=pltpu.SMEM)
LIMIT = 62 * 1024 * 1024
BLOCKS = [(i, j) for i in range(4) for j in range(i, 4)]
NT = (((1,), (1,)), ((), ()))
TN = (((0,), (0,)), ((), ()))


def dot(a, b, dims=(((1,), (0,)), ((), ())), precision=None):
    return lax.dot_general(a, b, dims, precision=precision, preferred_element_type=jnp.float32)


def iota(shape, axis):
    return lax.broadcasted_iota(jnp.int32, shape, axis)


def thirds(x):
    high = x.astype(jnp.bfloat16)
    rest = x - high.astype(jnp.float32)
    mid = rest.astype(jnp.bfloat16)
    low = (rest - mid.astype(jnp.float32)).astype(jnp.bfloat16)
    return high, mid, low


def add_tree(terms):
    while len(terms) > 1:
        terms = [terms[k] + terms[k + 1] if k + 1 < len(terms) else terms[k] for k in range(0, len(terms), 2)]
    return terms[0]


def stacked_thirds(x):
    high, mid, low = thirds(x)
    row = iota((16, x.shape[1]), 0)
    wide = lambda part: jnp.broadcast_to(part.astype(jnp.float32), row.shape)
    parts = jnp.where(row == 0, wide(high), jnp.where(row == 1, wide(mid), jnp.where(row == 2, wide(low), 0.0)))
    return parts.astype(jnp.bfloat16)


def remote(src, dst, send, recv, device):
    return pltpu.make_async_remote_copy(
        src_ref=src, dst_ref=dst, send_sem=send, recv_sem=recv, device_id=device, device_id_type=MESH)


def position():
    return lax.axis_index("tile"), lax.axis_index("rep")


def request_rows(owner, local, anchor, frac_x, frac_y, label):
    named = (iota((OWNERS, FIXES), 0) == owner).astype(jnp.float32)
    named_b = named.astype(jnp.bfloat16)
    earlier = (iota((FIXES, FIXES), 0) < iota((FIXES, FIXES), 1)).astype(jnp.float32).astype(jnp.bfloat16)
    before = dot(named_b, earlier)
    slot = jnp.sum(before * named, axis=0, keepdims=True)
    at = iota((SLOTS, FIXES), 0).astype(jnp.float32) == slot
    fields = [field.astype(jnp.float32) for field in (local, anchor, frac_x, frac_y, label + 1)]
    spread = [jnp.where(at, field, 0.0) for field in fields] + [jnp.zeros((8, FIXES), jnp.float32)]
    spread = jnp.concatenate(spread, axis=0).astype(jnp.bfloat16)
    return dot(named_b, spread, NT), slot


def other_owners(tile):
    x, z = lax.div(tile, DEEP), lax.rem(tile, DEEP)
    reach = lambda step, size: min(step, size - step)
    steps = [(dx, dz) for dx in range(4) for dz in range(DEEP) if dx or dz]
    for dx, dz in sorted(steps, key=lambda step: -(reach(step[0], 4) + reach(step[1], DEEP))):
        yield lax.rem(x + dx, 4) * DEEP + lax.rem(z + dz, DEEP)


def greet_tile(barrier, tile, rep):
    for peer in other_owners(tile):
        pl.semaphore_signal(barrier, inc=1, device_id=(peer, rep), device_id_type=MESH)


def send_some(peers, tile, rep, out, came, send_sem, recv_sem):
    for peer in peers:
        remote(out.at[peer], came.at[tile], send_sem, recv_sem, (peer, rep)).start()


def all_messages(tile, rep, out, came, send_sem, recv_sem):
    many = pl.ds(0, OWNERS - 1)
    return remote(out.at[many], came.at[many], send_sem, recv_sem, (lax.rem(tile + 1, OWNERS), rep))


def swap_rows_and_tiles(raster, turned):
    group = iota((LAYERS, 128), 1) // 16
    for half in range(2):
        for part in range(2):
            held = [raster[8 * part + t, :, half * 128:(half + 1) * 128].astype(jnp.float32) for t in range(8)]
            for step in (1, 2, 4):
                upper = (group // step) % 2 == 1
                for t in range(8):
                    if t & step == 0:
                        a, b = held[t], held[t | step]
                        held[t] = jnp.where(upper, pltpu.roll(b, 16 * step, 1), a)
                        held[t | step] = jnp.where(upper, b, pltpu.roll(a, 128 - 16 * step, 1))
            for r in range(8):
                row = 8 * half + r
                turned[row * 64:(row + 1) * 64, part * 128:(part + 1) * 128] = held[r].astype(jnp.bfloat16)


def expand(values):
    shape = (LAYERS, SPLINES, values.shape[1])
    spread = jnp.broadcast_to(values[:, None, :], shape)
    knots = 0.5 * (iota(shape, 1).astype(jnp.float32) - 0.5 * (SPLINES - 1))
    bump = jnp.maximum(1.0 - jnp.abs(spread - knots) * (1.0 / 0.75), 0.0)
    return (bump * bump * bump).reshape(BASIS, values.shape[1]).astype(jnp.bfloat16)


def form_terms(codes, beta, packed, coded, rows_out, turned, scaled, resid, panel_done):
    beta_parts = stacked_thirds(beta[...])

    def block(at):
        def field(f):
            return jnp.concatenate([codes[pl.ds(f * SLOTS + 2 * at, 1), :], codes[pl.ds(f * SLOTS + 2 * at + 1, 1), :]], axis=1)

        local, anchor, frac_x, frac_y, mark = [field(f) for f in range(5)]
        row = jnp.floor((anchor + 0.5) * (1.0 / 15.0))
        cell = local * 16.0 + (anchor - 15.0 * row)
        lane = iota((256, 256), 0).astype(jnp.float32)
        weight_x = jnp.where(lane == cell, 256.0 - frac_x, 0.0) + jnp.where(lane == cell + 1.0, frac_x, 0.0)
        along = dot(turned[...], weight_x.astype(jnp.bfloat16))
        values = None
        for r in range(16):
            weight_y = jnp.where(row == float(r), 256.0 - frac_y, 0.0) + jnp.where(row == float(r - 1), frac_y, 0.0)
            term = weight_y * along[r * 64:(r + 1) * 64]
            values = term if values is None else values + term
        values = values * (1.0 / 65536.0)
        lanes = pl.ds(at * 256, 256)
        coded[:, lanes] = jnp.floor(jnp.clip(values, -REACH, REACH) * STEPS + 0.5).astype(jnp.int32)
        rows = expand(values)
        rows_out[:, lanes] = rows
        eta = jnp.sum(dot(beta_parts, rows), axis=0, keepdims=True)
        live = (mark > 0.5).astype(jnp.float32)
        outcome = mark - 1.0
        prob = 1.0 / (1.0 + jnp.exp(-eta))
        weight = prob * (1.0 - prob) * live
        scaled[:, lanes] = (jnp.sqrt(weight) * rows.astype(jnp.float32)).astype(jnp.bfloat16)
        resid[:, lanes] = stacked_thirds(weight * eta + (outcome - prob) * live)

    for at in range(6):
        block(at)
    target = jnp.sum(dot(resid[...], rows_out[...], NT), axis=0, keepdims=True)
    for spare in range(GRAM_TILES, 2 * USED * 3):
        packed[spare // 3, spare % 3 * 8:spare % 3 * 8 + 8, :] = jnp.zeros((8, 128), jnp.float32)
    for part in range(4):
        packed[GRAM_TILES // 3, TARGET_ROW + part:TARGET_ROW + part + 1, :] = target[:, part * 128:(part + 1) * 128]
    tile = 0
    for i in range(4):
        panel = dot(scaled[i * 128:(i + 1) * 128, :], scaled[i * 128:, :], NT)
        for j in range(i, 4):
            for r in range(16):
                packed[tile // 3, tile % 3 * 8:tile % 3 * 8 + 8, :] = panel[r * 8:r * 8 + 8, (j - i) * 128:(j - i + 1) * 128]
                tile += 1
        panel_done(tile // 6 if i < 3 else GROUP)


def add_up(place, packed, mate_in, paired, group_in, mine, level_in, whole, result, sems, while_down):
    s_mate, r_mate, s_group, r_group, s_level, r_level, s_wide, r_wide, s_last, r_last = sems
    me, core, pair, mate, chip, level = place
    peer = chip(lax.rem(me + 1, GROUP))
    most = pl.ds(0, GROUP - 1)
    others = [lax.rem(pair + step, LEVELS) for step in (4, 3, 5, 2, 6, 1, 7)]
    around = [lax.rem(me + step, GROUP) for step in range(1, GROUP)]
    sent = [0]

    def to_mate(p):
        return remote(packed.at[2 * p + 1 - core], mate_in.at[p], s_mate, r_mate.at[p], mate)

    def back_chip(p, slot):
        return remote(whole, result.at[2 * slot + core], s_wide, r_wide.at[slot], chip(p))

    def back_mate(p, whose):
        chunk = result.at[2 * p + whose]
        return remote(chunk, chunk, s_last, r_last.at[p], mate)

    def all_group():
        return remote(paired.at[most], group_in.at[most], s_group, r_group, peer)

    def send_ready(stop):
        for p in range(sent[0], min(stop, USED)):
            to_mate(p).start()
        sent[0] = stop

    def pair_sum(p):
        to_mate(p).wait_recv()
        paired[p] = packed[2 * p + core] + mate_in[p]

    def forward(p):
        @pl.when(p != me)
        def _():
            back_chip(p, p).wait_recv()
            back_mate(p, core).start()

    def to_chip(p):
        return remote(paired.at[p], group_in.at[me], s_group, r_group, chip(p))

    def down_and_first(first):
        for step in range(1, USED):
            p = lax.rem(me + step, USED)
            pair_sum(p)
            to_chip(p).start()
        last = lax.rem(me, USED)
        pair_sum(last)

        @pl.when(me >= USED)
        def _():
            to_chip(last).start()

        while_down()

        @pl.when(me < USED)
        def _():
            group_in[me] = paired[me]
            all_group().wait_recv()
            mine[...] = add_tree([group_in[p] for p in range(GROUP)])
            for k in others:
                remote(mine, level_in.at[pair], s_level.at[k], r_level.at[pair], level(k)).start()
            level_in[pair] = mine[...]
            for k in others:
                remote(mine, level_in.at[k], s_level.at[k], r_level.at[k], level(k)).wait_recv()
            total = add_tree([level_in[k] for k in range(LEVELS)])
            whole[...] = total
            result[2 * me + core] = total
            for p in around:
                back_chip(p, me).start()
            back_mate(me, core).start()

        for p in range(first):
            forward(p)
        for p in range(first):
            back_mate(p, 1 - core).wait_recv()

    def forward_rest(start, stop):
        def one(p, _):
            forward(p)
            return 0

        lax.fori_loop(start, stop, one, 0)

    def wait_rest(start):
        def one(p, _):
            back_mate(p, 1 - core).wait_recv()
            return 0

        lax.fori_loop(start, USED, one, 0)

    def sent_bytes(count, sem):
        some = result.at[pl.ds(0, count)]
        remote(some, some, sem, sem, peer).wait_send()

    def settle():
        sent_bytes(USED, s_mate)
        sent_bytes(USED - 1, s_group)
        sent_bytes(USED, s_last)

        @pl.when(me >= USED)
        def _():
            sent_bytes(1, s_group)

        @pl.when(me < USED)
        def _():
            for k in others:
                remote(mine, level_in.at[k], s_level.at[k], r_level.at[k], level(k)).wait_send()
            sent_bytes(GROUP - 1, s_wide)

    return send_ready, down_and_first, forward_rest, wait_rest, settle


def pack_values(coded, out):
    for t in range(3):
        words = []
        for r in (2 * t, 2 * t + 1):
            low, high = coded[:, r * 128:(r + 1) * 128], coded[:, (r + 6) * 128:(r + 7) * 128]
            words.append((low & 65535) | (high << 16))
        turned = jnp.concatenate(words, axis=0).T
        for k in range(OWNERS):
            out[k, 2 * t:2 * t + 1, :] = turned[k:k + 1, :]
            out[k, 2 * t + 1:2 * t + 2, :] = turned[OWNERS + k:OWNERS + k + 1, :]


def unpack_words(came, bytes_out, t):
    words = jnp.concatenate([came[k, 2 * t + half:2 * t + half + 1, :] for half in range(2) for k in range(OWNERS)], axis=0).T
    for which, codes in enumerate(((words << 16) >> 16, words >> 16)):
        for r in range(2):
            code = codes[r * 64:(r + 1) * 64, :]
            upper, lower = code >> 8, code & 255
            both = jnp.concatenate([upper, lower], axis=0).astype(jnp.float32).astype(jnp.bfloat16)
            block = 6 * which + 2 * t + r
            bytes_out[:, block * 128:(block + 1) * 128] = both


def values_of_fixes(bytes_in, owner, slot):
    second = slot >= 12.0
    key = jnp.where(second, (slot - 12.0) * 128.0 + 64.0, slot * 128.0) + owner.astype(jnp.float32)
    place = iota((OWNERS * SLOTS, key.shape[1]), 0).astype(jnp.float32)
    picked = dot(bytes_in[...], (place == key).astype(jnp.float32).astype(jnp.bfloat16))
    return (picked[:LAYERS] * 256.0 + picked[LAYERS:]) * (1.0 / STEPS)


def reciprocal(x):
    guess = pltpu.reciprocal(x, approx=True)
    return guess * (2.0 - x * guess)


def six_left(x):
    high, mid, low = thirds(x)
    return jnp.concatenate([high, high, high, mid, mid, low], axis=1)


def six_right(x):
    high, mid, low = thirds(x)
    return jnp.concatenate([high, mid, low, high, mid, high], axis=0)


def invert(tiles, chores):
    tiles, chores = list(tiles), list(chores)
    share = -(-len(chores) // 15)
    lane = iota((8, 128), 1)
    row = iota((8, 128), 0)

    def take(tile, m):
        return jnp.broadcast_to(tile[m:m + 1, :], (8, 128))

    def column(tile, at):
        return jnp.broadcast_to(tile[:, at:at + 1], (8, 128))

    for b in range(16):
        inside = (lane // 8) == b
        columns = [column(tiles[b], 8 * b + m) for m in range(8)]
        lead = jnp.where(inside, jnp.where(lane - 8 * b == row, 1.0, 0.0), tiles[b])
        for m in range(0, 8, 2):
            p, q, r = take(columns[m], m), take(columns[m + 1], m), take(columns[m + 1], m + 1)
            scale = reciprocal(p * r - q * q)
            is_first, is_second = row == m, row == m + 1

            def sweep(tile):
                first, second = take(tile, m), take(tile, m + 1)
                first, second = r * first - q * second, p * second - q * first
                rest = tile - (columns[m] * first + columns[m + 1] * second) * scale
                return jnp.where(is_first, first * scale, jnp.where(is_second, second * scale, rest))

            later = [sweep(columns[k]) for k in range(m + 2, 8)]
            lead = sweep(lead)
            columns = columns[:m + 2] + later
        taken = [take(lead, m) for m in range(8)]
        for i in [(b + 1 + s) % 16 for s in range(15)]:
            terms = [column(tiles[i], 8 * b + m) * taken[m] for m in range(8)]
            tiles[i] = jnp.where(inside, 0.0, tiles[i]) - add_tree(terms)
        tiles[b] = lead
        for chore in chores[b * share:(b + 1) * share]:
            chore()
    return tiles


def second_difference():
    i, j = iota((8, 128), 0), iota((8, 128), 1) % 8
    inner = jnp.zeros((8, 128), jnp.float32)

    def entry(at, r):
        return jnp.where(at == r, 1.0, 0.0) - jnp.where(at == r + 1, 2.0, 0.0) + jnp.where(at == r + 2, 1.0, 0.0)

    for r in range(SPLINES - 2):
        inner = inner + entry(i, r) * entry(j, r)
    return inner


def solve_system(sums, smooth, beta_new, system, spread, first_chores, late_chores):
    count = 1.0 / (FIXES * 512.0)
    lane, row = iota((8, 128), 1), iota((8, 128), 0)
    inner = second_difference()

    def assemble(number):
        i, j = BLOCKS[number]
        for r in range(16):
            tile = 16 * number + r
            value = sums[tile // 3, tile % 3 * 8:tile % 3 * 8 + 8, :] * count
            if i == j:
                value = value + jnp.where(lane // 8 == r, smooth[16 * i + r] * inner, 0.0)
                value = value + jnp.where(lane == row + 8 * r, RIDGE, 0.0)
            system[i, r * 8:r * 8 + 8, j * 128:(j + 1) * 128] = value

    def assemble_right():
        for part in range(4):
            line = sums[GRAM_TILES // 3, TARGET_ROW + part:TARGET_ROW + part + 1, :] * count
            system[part, :, 512:640] = jnp.broadcast_to(line, (128, 128)).T

    assemble(0)
    def spread_of(k, inverse, start, stop):
        part = dot(inverse, six_right(system[k, :, start:stop]))
        system[k, :, start:stop] = part
        spread[:, start:stop] = six_right(part)

    def eliminate(i, left, start, stop):
        system[i, :, start:stop] = system[i, :, start:stop] - dot(left, spread[:, start:stop])

    pending = first_chores + [functools.partial(assemble, number) for number in range(1, 10)] + [assemble_right]
    for k in range(4):
        diagonal = [system[k, r * 8:r * 8 + 8, k * 128:(k + 1) * 128] for r in range(16)]
        inverse = six_left(jnp.concatenate(invert(diagonal, pending), axis=0))
        near = (k + 1) * 128
        lefts = {i: six_left(system[k, :, i * 128:(i + 1) * 128].T) for i in range(k + 1, 4)}
        lefts.update({i: six_left(system[i, :, k * 128:(k + 1) * 128]) for i in range(k)})
        spread_of(k, inverse, near, near + 128)
        pending = []
        if k < 3:
            eliminate(k + 1, lefts[k + 1], near, near + 128)
            pending.append(functools.partial(spread_of, k, inverse, near + 128, 640))
            pending.append(functools.partial(eliminate, k + 1, lefts[k + 1], near + 128, 640))
            for i in range(k + 2, 4):
                pending.append(functools.partial(eliminate, i, lefts[i], i * 128, 640))
            for i in range(k):
                pending.append(functools.partial(eliminate, i, lefts[i], near, 640))
        else:
            for i in range(k):
                eliminate(i, lefts[i], 512, 640)
        if k == 2:
            pending += late_chores
    for k in range(4):
        beta_new[:, k * 128:(k + 1) * 128] = system[k, :, 512:640].T[0:1, :]


def step_kernel(owner, local, anchor, frac_x, frac_y, label, raster, beta, smooth, beta_new, eta_new,
                lines, raster_in, beta_in, out_codes, came, codes, turned, rows, scaled, resid, coded,
                packed, mate_in, paired, group_in, mine, level_in, whole, result,
                out_values, came_values, value_bytes, own_rows, slot_row, system, spread,
                loads, send_codes, recv_codes, send_values, recv_values, *sems):
    tile, rep = position()
    x, z = lax.div(tile, DEEP), lax.rem(tile, DEEP)
    y, core = lax.div(rep, 2), lax.rem(rep, 2)
    pair, low = lax.div(z, 2), lax.rem(z, 2)
    me = (x * 4 + y) * 2 + low
    mate = (tile, rep + 1 - 2 * core)

    def chip(p):
        return (lax.div(p, 8) * DEEP + pair * 2 + lax.rem(p, 2), lax.rem(lax.div(p, 2), 4) * 2 + core)

    def level(k):
        return (x * DEEP + k * 2 + low, rep)

    barrier = pltpu.get_barrier_semaphore()
    greet_tile(barrier, tile, rep)
    pl.semaphore_signal(barrier, inc=1, device_id=mate, device_id_type=MESH)

    def greet(step, _):
        other_y = lax.rem(y + 1 + lax.rem(step, 3), 4)
        rest = lax.div(step, 3)
        device = (lax.div(rest, 2) * DEEP + pair * 2 + lax.rem(rest, 2), other_y * 2 + core)
        pl.semaphore_signal(barrier, inc=1, device_id=device, device_id_type=MESH)
        return 0

    lax.fori_loop(0, 24, greet, 0)

    arguments = [(source, lines.at[k]) for k, source in enumerate((owner, local, anchor, frac_x, frac_y, label))]
    arguments += [(raster, raster_in), (beta, beta_in)]
    copies = [pltpu.make_async_copy(source, target, loads.at[k]) for k, (source, target) in enumerate(arguments)]
    for copy in copies:
        copy.start()
    for copy in copies[:6]:
        copy.wait()
    message, slot = request_rows(*[lines[k] for k in range(6)])
    slot_row[...] = slot
    for k in range(OWNERS):
        out_codes[k] = message[k:k + 1, :]
    copies[6].wait()
    copies[7].wait()
    swap_rows_and_tiles(raster_in, turned)
    pl.semaphore_wait(barrier, OWNERS - 1 + 24 + 1)

    codes_sent = (tile, rep, out_codes, came, send_codes, recv_codes)
    came[tile] = out_codes[tile]
    send_some(other_owners(tile), *codes_sent)
    all_messages(*codes_sent).wait_recv()
    arrived = jnp.concatenate([came[k] for k in range(OWNERS)], axis=0)
    codes[...] = jnp.concatenate([arrived, pltpu.roll(arrived, 128 - 12, 1)], axis=0).T
    values_sent = (tile, rep, out_values, came_values, send_values, recv_values)
    send_ready, down_and_first, forward_rest, wait_rest, settle = add_up(
        (me, core, pair, mate, chip, level), packed, mate_in, paired, group_in, mine, level_in, whole, result, sems,
        lambda: pack_values(coded, out_values))
    form_terms(codes, beta_in, packed, coded, rows, turned, scaled, resid, send_ready)
    down_and_first(FIRST)

    def place_rows(part):
        values = values_of_fixes(value_bytes, lines[0, :, part * 128:(part + 1) * 128], slot_row[:, part * 128:(part + 1) * 128])
        own_rows[:, part * 128:(part + 1) * 128] = expand(values)

    peers = list(other_owners(tile))
    half = (FIRST + USED) // 2
    first_chores = [functools.partial(forward_rest, FIRST, half), functools.partial(forward_rest, half, USED)]
    first_chores += [functools.partial(send_some, peers[k:k + 21], *values_sent) for k in range(0, OWNERS - 1, 21)]
    first_chores += [functools.partial(wait_rest, FIRST)]

    def settle_all():
        settle()
        all_messages(*codes_sent).wait_send()
        came_values[tile] = out_values[tile]
        all_messages(*values_sent).wait_recv()

    chores = [settle_all]
    chores += [functools.partial(unpack_words, came_values, value_bytes, t) for t in range(3)]
    chores += [functools.partial(place_rows, part) for part in range(4)]
    solve_system(result, smooth, beta_new, system, spread, first_chores, chores)
    eta_new[...] = jnp.sum(dot(stacked_thirds(beta_new[...]), own_rows[...]), axis=0, keepdims=True)
    all_messages(*values_sent).wait_send()


def step(lines, raster, beta, smooth):
    f32, bf16, i32 = jnp.float32, jnp.bfloat16, jnp.int32
    one = pltpu.SemaphoreType.DMA
    group = pltpu.SemaphoreType.DMA((GROUP,))
    deep = pltpu.SemaphoreType.DMA((LEVELS,))
    chunks = pltpu.VMEM((GROUP, ROWS, 128), f32)
    chunk = pltpu.VMEM((ROWS, 128), f32)
    served = OWNERS * SLOTS
    return pl.pallas_call(
        step_kernel,
        out_shape=(jax.ShapeDtypeStruct((1, BASIS), f32), jax.ShapeDtypeStruct((1, FIXES), f32)),
        in_specs=[pl.BlockSpec(memory_space=pltpu.HBM)] * 8 + [SMEM],
        out_specs=(VMEM, VMEM),
        scratch_shapes=[
            pltpu.VMEM((6, 1, FIXES), i32),
            pltpu.VMEM((16, LAYERS, 256), bf16),
            pltpu.VMEM((1, BASIS), f32),
            pltpu.VMEM((OWNERS, 1, 128), f32),
            pltpu.VMEM((OWNERS, 1, 128), f32),
            pltpu.VMEM((128, 128), f32),
            pltpu.VMEM((1024, 256), bf16),
            pltpu.VMEM((BASIS, served), bf16),
            pltpu.VMEM((BASIS, served), bf16),
            pltpu.VMEM((16, served), bf16),
            pltpu.VMEM((LAYERS, served), i32),
            pltpu.VMEM((2 * GROUP, ROWS, 128), f32),
            chunks, chunks, chunks,
            chunk,
            pltpu.VMEM((LEVELS, ROWS, 128), f32),
            chunk,
            pltpu.VMEM((2 * GROUP, ROWS, 128), f32),
            pltpu.VMEM((OWNERS, 6, 128), i32),
            pltpu.VMEM((OWNERS, 6, 128), i32),
            pltpu.VMEM((128, served), bf16),
            pltpu.VMEM((BASIS, FIXES), bf16),
            pltpu.VMEM((1, FIXES), f32),
            pltpu.VMEM((4, 128, BASIS + 128), f32),
            pltpu.VMEM((768, BASIS + 128), bf16),
            pltpu.SemaphoreType.DMA((8,)),
            one, one, one, one,
            one, group, one, one, deep, deep, one, group, one, group,
        ],
        compiler_params=pltpu.CompilerParams(collective_id=0, has_side_effects=True, vmem_limit_bytes=LIMIT),
    )(*lines, raster, beta, smooth)


def shards(owner, tile_local, anchor, frac_x, frac_y, label, raster, beta, smooth):
    lines = [array.reshape(1, FIXES) for array in (owner, tile_local, anchor, frac_x, frac_y, label)]
    beta_new, eta_new = step(lines, raster, beta.reshape(1, BASIS), smooth)
    return beta_new.reshape(BASIS), eta_new.reshape(FIXES)


def solution(mesh):
    fixes = P(("tile", "rep"))
    placed = (P(("tile", "rep"), None), fixes, fixes, fixes, fixes, fixes, P("tile", None, None), P(), P())
    return jax.shard_map(shards, mesh=mesh, in_specs=placed, out_specs=(P(), fixes), check_vma=False)
```

```python
import functools

import jax
import jax.numpy as jnp
from jax import lax
from jax.experimental import pallas as pl
from jax.experimental.pallas import tpu as pltpu
from jax.sharding import PartitionSpec as P

SPLINES = 8
RIDGE = 0.002
LAYERS = 64
BASIS = 512
FIXES = 512
SLOTS = 24
OWNERS = 64
DEEP = 16
GROUP = 32
LEVELS = 8
ROWS = 24
GRAM_TILES = 160
TARGET_ROW = GRAM_TILES % 3 * 8
USED = 27
FIRST = 3
REACH = 2.5
STEPS = 13104.0
MESH = pl.DeviceIdType.MESH
HIGHEST = lax.Precision.HIGHEST
VMEM = pl.BlockSpec(memory_space=pltpu.VMEM)
SMEM = pl.BlockSpec(memory_space=pltpu.SMEM)
LIMIT = 62 * 1024 * 1024
BLOCKS = [(i, j) for i in range(4) for j in range(i, 4)]
NT = (((1,), (1,)), ((), ()))
TN = (((0,), (0,)), ((), ()))


def dot(a, b, dims=(((1,), (0,)), ((), ())), precision=None):
    return lax.dot_general(a, b, dims, precision=precision, preferred_element_type=jnp.float32)


def iota(shape, axis):
    return lax.broadcasted_iota(jnp.int32, shape, axis)


def thirds(x):
    high = x.astype(jnp.bfloat16)
    rest = x - high.astype(jnp.float32)
    mid = rest.astype(jnp.bfloat16)
    low = (rest - mid.astype(jnp.float32)).astype(jnp.bfloat16)
    return high, mid, low


def add_tree(terms):
    while len(terms) > 1:
        terms = [terms[k] + terms[k + 1] if k + 1 < len(terms) else terms[k] for k in range(0, len(terms), 2)]
    return terms[0]


def stacked_thirds(x):
    high, mid, low = thirds(x)
    row = iota((16, x.shape[1]), 0)
    wide = lambda part: jnp.broadcast_to(part.astype(jnp.float32), row.shape)
    parts = jnp.where(row == 0, wide(high), jnp.where(row == 1, wide(mid), jnp.where(row == 2, wide(low), 0.0)))
    return parts.astype(jnp.bfloat16)


def remote(src, dst, send, recv, device):
    return pltpu.make_async_remote_copy(
        src_ref=src, dst_ref=dst, send_sem=send, recv_sem=recv, device_id=device, device_id_type=MESH)


def position():
    return lax.axis_index("tile"), lax.axis_index("rep")


def request_rows(owner, local, anchor, frac_x, frac_y, label):
    named = (iota((OWNERS, FIXES), 0) == owner).astype(jnp.float32)
    named_b = named.astype(jnp.bfloat16)
    earlier = (iota((FIXES, FIXES), 0) < iota((FIXES, FIXES), 1)).astype(jnp.float32).astype(jnp.bfloat16)
    before = dot(named_b, earlier)
    slot = jnp.sum(before * named, axis=0, keepdims=True)
    at = iota((SLOTS, FIXES), 0).astype(jnp.float32) == slot
    fields = [field.astype(jnp.float32) for field in (local, anchor, frac_x, frac_y, label + 1)]
    spread = [jnp.where(at, field, 0.0) for field in fields] + [jnp.zeros((8, FIXES), jnp.float32)]
    spread = jnp.concatenate(spread, axis=0).astype(jnp.bfloat16)
    return dot(named_b, spread, NT), slot


def other_owners(tile):
    x, z = lax.div(tile, DEEP), lax.rem(tile, DEEP)
    reach = lambda step, size: min(step, size - step)
    steps = [(dx, dz) for dx in range(4) for dz in range(DEEP) if dx or dz]
    for dx, dz in sorted(steps, key=lambda step: -(reach(step[0], 4) + reach(step[1], DEEP))):
        yield lax.rem(x + dx, 4) * DEEP + lax.rem(z + dz, DEEP)


def greet_tile(barrier, tile, rep):
    for peer in other_owners(tile):
        pl.semaphore_signal(barrier, inc=1, device_id=(peer, rep), device_id_type=MESH)


def send_some(peers, tile, rep, out, came, send_sem, recv_sem):
    for peer in peers:
        remote(out.at[peer], came.at[tile], send_sem, recv_sem, (peer, rep)).start()


def all_messages(tile, rep, out, came, send_sem, recv_sem):
    many = pl.ds(0, OWNERS - 1)
    return remote(out.at[many], came.at[many], send_sem, recv_sem, (lax.rem(tile + 1, OWNERS), rep))


def swap_rows_and_tiles(raster, turned):
    group = iota((LAYERS, 128), 1) // 16
    for half in range(2):
        for part in range(2):
            held = [raster[8 * part + t, :, half * 128:(half + 1) * 128].astype(jnp.float32) for t in range(8)]
            for step in (1, 2, 4):
                upper = (group // step) % 2 == 1
                for t in range(8):
                    if t & step == 0:
                        a, b = held[t], held[t | step]
                        held[t] = jnp.where(upper, pltpu.roll(b, 16 * step, 1), a)
                        held[t | step] = jnp.where(upper, b, pltpu.roll(a, 128 - 16 * step, 1))
            for r in range(8):
                row = 8 * half + r
                turned[row * 64:(row + 1) * 64, part * 128:(part + 1) * 128] = held[r].astype(jnp.bfloat16)


def expand(values):
    shape = (LAYERS, SPLINES, values.shape[1])
    spread = jnp.broadcast_to(values[:, None, :], shape)
    knots = 0.5 * (iota(shape, 1).astype(jnp.float32) - 0.5 * (SPLINES - 1))
    bump = jnp.maximum(1.0 - jnp.abs(spread - knots) * (1.0 / 0.75), 0.0)
    return (bump * bump * bump).reshape(BASIS, values.shape[1]).astype(jnp.bfloat16)


def form_terms(codes, beta, packed, coded, rows_out, turned, scaled, resid, panel_done):
    beta_parts = stacked_thirds(beta[...])

    def block(at):
        def field(f):
            return jnp.concatenate([codes[pl.ds(f * SLOTS + 2 * at, 1), :], codes[pl.ds(f * SLOTS + 2 * at + 1, 1), :]], axis=1)

        local, anchor, frac_x, frac_y, mark = [field(f) for f in range(5)]
        row = jnp.floor((anchor + 0.5) * (1.0 / 15.0))
        cell = local * 16.0 + (anchor - 15.0 * row)
        lane = iota((256, 256), 0).astype(jnp.float32)
        weight_x = jnp.where(lane == cell, 256.0 - frac_x, 0.0) + jnp.where(lane == cell + 1.0, frac_x, 0.0)
        along = dot(turned[...], weight_x.astype(jnp.bfloat16))
        values = None
        for r in range(16):
            weight_y = jnp.where(row == float(r), 256.0 - frac_y, 0.0) + jnp.where(row == float(r - 1), frac_y, 0.0)
            term = weight_y * along[r * 64:(r + 1) * 64]
            values = term if values is None else values + term
        values = values * (1.0 / 65536.0)
        lanes = pl.ds(at * 256, 256)
        coded[:, lanes] = jnp.floor(jnp.clip(values, -REACH, REACH) * STEPS + 0.5).astype(jnp.int32)
        rows = expand(values)
        rows_out[:, lanes] = rows
        eta = jnp.sum(dot(beta_parts, rows), axis=0, keepdims=True)
        live = (mark > 0.5).astype(jnp.float32)
        outcome = mark - 1.0
        prob = 1.0 / (1.0 + jnp.exp(-eta))
        weight = prob * (1.0 - prob) * live
        scaled[:, lanes] = (jnp.sqrt(weight) * rows.astype(jnp.float32)).astype(jnp.bfloat16)
        resid[:, lanes] = stacked_thirds(weight * eta + (outcome - prob) * live)

    for at in range(6):
        block(at)
    target = jnp.sum(dot(resid[...], rows_out[...], NT), axis=0, keepdims=True)
    for spare in range(GRAM_TILES, 2 * USED * 3):
        packed[spare // 3, spare % 3 * 8:spare % 3 * 8 + 8, :] = jnp.zeros((8, 128), jnp.float32)
    for part in range(4):
        packed[GRAM_TILES // 3, TARGET_ROW + part:TARGET_ROW + part + 1, :] = target[:, part * 128:(part + 1) * 128]
    tile = 0
    for i in range(4):
        panel = dot(scaled[i * 128:(i + 1) * 128, :], scaled[i * 128:, :], NT)
        for j in range(i, 4):
            for r in range(16):
                packed[tile // 3, tile % 3 * 8:tile % 3 * 8 + 8, :] = panel[r * 8:r * 8 + 8, (j - i) * 128:(j - i + 1) * 128]
                tile += 1
        panel_done(tile // 6 if i < 3 else GROUP)


def add_up(place, packed, mate_in, paired, group_in, mine, level_in, whole, result, sems, while_down):
    s_mate, r_mate, s_group, r_group, s_level, r_level, s_wide, r_wide, s_last, r_last = sems
    me, core, pair, mate, chip, level = place
    peer = chip(lax.rem(me + 1, GROUP))
    most = pl.ds(0, GROUP - 1)
    others = [lax.rem(pair + step, LEVELS) for step in (4, 3, 5, 2, 6, 1, 7)]
    around = [lax.rem(me + step, GROUP) for step in range(1, GROUP)]
    sent = [0]

    def to_mate(p):
        return remote(packed.at[2 * p + 1 - core], mate_in.at[p], s_mate, r_mate.at[p], mate)

    def back_chip(p, slot):
        return remote(whole, result.at[2 * slot + core], s_wide, r_wide.at[slot], chip(p))

    def back_mate(p, whose):
        chunk = result.at[2 * p + whose]
        return remote(chunk, chunk, s_last, r_last.at[p], mate)

    def all_group():
        return remote(paired.at[most], group_in.at[most], s_group, r_group, peer)

    def send_ready(stop):
        for p in range(sent[0], min(stop, USED)):
            to_mate(p).start()
        sent[0] = stop

    def pair_sum(p):
        to_mate(p).wait_recv()
        paired[p] = packed[2 * p + core] + mate_in[p]

    def forward(p):
        @pl.when(p != me)
        def _():
            back_chip(p, p).wait_recv()
            back_mate(p, core).start()

    def to_chip(p):
        return remote(paired.at[p], group_in.at[me], s_group, r_group, chip(p))

    def down_and_first(first):
        for step in range(1, USED):
            p = lax.rem(me + step, USED)
            pair_sum(p)
            to_chip(p).start()
        last = lax.rem(me, USED)
        pair_sum(last)

        @pl.when(me >= USED)
        def _():
            to_chip(last).start()

        while_down()

        @pl.when(me < USED)
        def _():
            group_in[me] = paired[me]
            all_group().wait_recv()
            mine[...] = add_tree([group_in[p] for p in range(GROUP)])
            for k in others:
                remote(mine, level_in.at[pair], s_level.at[k], r_level.at[pair], level(k)).start()
            level_in[pair] = mine[...]
            for k in others:
                remote(mine, level_in.at[k], s_level.at[k], r_level.at[k], level(k)).wait_recv()
            total = add_tree([level_in[k] for k in range(LEVELS)])
            whole[...] = total
            result[2 * me + core] = total
            for p in around:
                back_chip(p, me).start()
            back_mate(me, core).start()

        for p in range(first):
            forward(p)
        for p in range(first):
            back_mate(p, 1 - core).wait_recv()

    def forward_rest(start, stop):
        def one(p, _):
            forward(p)
            return 0

        lax.fori_loop(start, stop, one, 0)

    def wait_rest(start):
        def one(p, _):
            back_mate(p, 1 - core).wait_recv()
            return 0

        lax.fori_loop(start, USED, one, 0)

    def sent_bytes(count, sem):
        some = result.at[pl.ds(0, count)]
        remote(some, some, sem, sem, peer).wait_send()

    def settle():
        sent_bytes(USED, s_mate)
        sent_bytes(USED - 1, s_group)
        sent_bytes(USED, s_last)

        @pl.when(me >= USED)
        def _():
            sent_bytes(1, s_group)

        @pl.when(me < USED)
        def _():
            for k in others:
                remote(mine, level_in.at[k], s_level.at[k], r_level.at[k], level(k)).wait_send()
            sent_bytes(GROUP - 1, s_wide)

    return send_ready, down_and_first, forward_rest, wait_rest, settle


def pack_values(coded, out):
    for t in range(3):
        words = []
        for r in (2 * t, 2 * t + 1):
            low, high = coded[:, r * 128:(r + 1) * 128], coded[:, (r + 6) * 128:(r + 7) * 128]
            words.append((low & 65535) | (high << 16))
        turned = jnp.concatenate(words, axis=0).T
        for k in range(OWNERS):
            out[k, 2 * t:2 * t + 1, :] = turned[k:k + 1, :]
            out[k, 2 * t + 1:2 * t + 2, :] = turned[OWNERS + k:OWNERS + k + 1, :]


def unpack_words(came, bytes_out, t):
    words = jnp.concatenate([came[k, 2 * t + half:2 * t + half + 1, :] for half in range(2) for k in range(OWNERS)], axis=0).T
    for which, codes in enumerate(((words << 16) >> 16, words >> 16)):
        for r in range(2):
            code = codes[r * 64:(r + 1) * 64, :]
            upper, lower = code >> 8, code & 255
            both = jnp.concatenate([upper, lower], axis=0).astype(jnp.float32).astype(jnp.bfloat16)
            block = 6 * which + 2 * t + r
            bytes_out[:, block * 128:(block + 1) * 128] = both


def values_of_fixes(bytes_in, owner, slot):
    second = slot >= 12.0
    key = jnp.where(second, (slot - 12.0) * 128.0 + 64.0, slot * 128.0) + owner.astype(jnp.float32)
    place = iota((OWNERS * SLOTS, key.shape[1]), 0).astype(jnp.float32)
    picked = dot(bytes_in[...], (place == key).astype(jnp.float32).astype(jnp.bfloat16))
    return (picked[:LAYERS] * 256.0 + picked[LAYERS:]) * (1.0 / STEPS)


def reciprocal(x):
    guess = pltpu.reciprocal(x, approx=True)
    return guess * (2.0 - x * guess)


def six_left(x):
    high, mid, low = thirds(x)
    return jnp.concatenate([high, high, high, mid, mid, low], axis=1)


def six_right(x):
    high, mid, low = thirds(x)
    return jnp.concatenate([high, mid, low, high, mid, high], axis=0)


def invert(tiles, chores):
    tiles, chores = list(tiles), list(chores)
    share = -(-len(chores) // 15)
    lane = iota((8, 128), 1)
    row = iota((8, 128), 0)

    def take(tile, m):
        return jnp.broadcast_to(tile[m:m + 1, :], (8, 128))

    def column(tile, at):
        return jnp.broadcast_to(tile[:, at:at + 1], (8, 128))

    for b in range(16):
        inside = (lane // 8) == b
        columns = [column(tiles[b], 8 * b + m) for m in range(8)]
        lead = jnp.where(inside, jnp.where(lane - 8 * b == row, 1.0, 0.0), tiles[b])
        for m in range(0, 8, 2):
            p, q, r = take(columns[m], m), take(columns[m + 1], m), take(columns[m + 1], m + 1)
            scale = reciprocal(p * r - q * q)
            is_first, is_second = row == m, row == m + 1

            def sweep(tile):
                first, second = take(tile, m), take(tile, m + 1)
                first, second = r * first - q * second, p * second - q * first
                rest = tile - (columns[m] * first + columns[m + 1] * second) * scale
                return jnp.where(is_first, first * scale, jnp.where(is_second, second * scale, rest))

            later = [sweep(columns[k]) for k in range(m + 2, 8)]
            lead = sweep(lead)
            columns = columns[:m + 2] + later
        taken = [take(lead, m) for m in range(8)]
        for i in [(b + 1 + s) % 16 for s in range(15)]:
            terms = [column(tiles[i], 8 * b + m) * taken[m] for m in range(8)]
            tiles[i] = jnp.where(inside, 0.0, tiles[i]) - add_tree(terms)
        tiles[b] = lead
        for chore in chores[b * share:(b + 1) * share]:
            chore()
    return tiles


def second_difference():
    i, j = iota((8, 128), 0), iota((8, 128), 1) % 8
    inner = jnp.zeros((8, 128), jnp.float32)

    def entry(at, r):
        return jnp.where(at == r, 1.0, 0.0) - jnp.where(at == r + 1, 2.0, 0.0) + jnp.where(at == r + 2, 1.0, 0.0)

    for r in range(SPLINES - 2):
        inner = inner + entry(i, r) * entry(j, r)
    return inner


def solve_system(sums, smooth, beta_new, system, spread, first_chores, late_chores):
    count = 1.0 / (FIXES * 512.0)
    lane, row = iota((8, 128), 1), iota((8, 128), 0)
    inner = second_difference()

    def assemble(number):
        i, j = BLOCKS[number]
        for r in range(16):
            tile = 16 * number + r
            value = sums[tile // 3, tile % 3 * 8:tile % 3 * 8 + 8, :] * count
            if i == j:
                value = value + jnp.where(lane // 8 == r, smooth[16 * i + r] * inner, 0.0)
                value = value + jnp.where(lane == row + 8 * r, RIDGE, 0.0)
            system[i, r * 8:r * 8 + 8, j * 128:(j + 1) * 128] = value

    def assemble_right():
        for part in range(4):
            line = sums[GRAM_TILES // 3, TARGET_ROW + part:TARGET_ROW + part + 1, :] * count
            system[part, :, 512:640] = jnp.broadcast_to(line, (128, 128)).T

    assemble(0)
    def spread_of(k, inverse, start, stop):
        part = dot(inverse, six_right(system[k, :, start:stop]))
        system[k, :, start:stop] = part
        spread[:, start:stop] = six_right(part)

    def eliminate(i, left, start, stop):
        system[i, :, start:stop] = system[i, :, start:stop] - dot(left, spread[:, start:stop])

    pending = first_chores + [functools.partial(assemble, number) for number in range(1, 10)] + [assemble_right]
    for k in range(4):
        diagonal = [system[k, r * 8:r * 8 + 8, k * 128:(k + 1) * 128] for r in range(16)]
        inverse = six_left(jnp.concatenate(invert(diagonal, pending), axis=0))
        near = (k + 1) * 128
        lefts = {i: six_left(system[k, :, i * 128:(i + 1) * 128].T) for i in range(k + 1, 4)}
        lefts.update({i: six_left(system[i, :, k * 128:(k + 1) * 128]) for i in range(k)})
        spread_of(k, inverse, near, near + 128)
        pending = []
        if k < 3:
            eliminate(k + 1, lefts[k + 1], near, near + 128)
            pending.append(functools.partial(spread_of, k, inverse, near + 128, 640))
            pending.append(functools.partial(eliminate, k + 1, lefts[k + 1], near + 128, 640))
            for i in range(k + 2, 4):
                pending.append(functools.partial(eliminate, i, lefts[i], i * 128, 640))
            for i in range(k):
                pending.append(functools.partial(eliminate, i, lefts[i], near, 640))
        else:
            for i in range(k):
                eliminate(i, lefts[i], 512, 640)
        if k == 2:
            pending += late_chores
    for k in range(4):
        beta_new[:, k * 128:(k + 1) * 128] = system[k, :, 512:640].T[0:1, :]


def step_kernel(owner, local, anchor, frac_x, frac_y, label, raster, beta, smooth, beta_new, eta_new,
                lines, raster_in, beta_in, smooth_in, out_codes, came, codes, turned, rows, scaled, resid, coded,
                packed, mate_in, paired, group_in, mine, level_in, whole, result,
                out_values, came_values, value_bytes, own_rows, slot_row, system, spread,
                loads, send_codes, recv_codes, send_values, recv_values, *sems):
    tile, rep = position()
    x, z = lax.div(tile, DEEP), lax.rem(tile, DEEP)
    y, core = lax.div(rep, 2), lax.rem(rep, 2)
    pair, low = lax.div(z, 2), lax.rem(z, 2)
    me = (x * 4 + y) * 2 + low
    mate = (tile, rep + 1 - 2 * core)

    def chip(p):
        return (lax.div(p, 8) * DEEP + pair * 2 + lax.rem(p, 2), lax.rem(lax.div(p, 2), 4) * 2 + core)

    def level(k):
        return (x * DEEP + k * 2 + low, rep)

    barrier = pltpu.get_barrier_semaphore()
    greet_tile(barrier, tile, rep)
    pl.semaphore_signal(barrier, inc=1, device_id=mate, device_id_type=MESH)

    def greet(step, _):
        other_y = lax.rem(y + 1 + lax.rem(step, 3), 4)
        rest = lax.div(step, 3)
        device = (lax.div(rest, 2) * DEEP + pair * 2 + lax.rem(rest, 2), other_y * 2 + core)
        pl.semaphore_signal(barrier, inc=1, device_id=device, device_id_type=MESH)
        return 0

    lax.fori_loop(0, 24, greet, 0)

    arguments = [(source, lines.at[k]) for k, source in enumerate((owner, local, anchor, frac_x, frac_y, label))]
    arguments += [(raster, raster_in), (beta, beta_in), (smooth, smooth_in)]
    copies = [pltpu.make_async_copy(source, target, loads.at[k]) for k, (source, target) in enumerate(arguments)]
    for copy in copies:
        copy.start()
    for copy in copies[:6]:
        copy.wait()
    message, slot = request_rows(*[lines[k] for k in range(6)])
    slot_row[...] = slot
    for k in range(OWNERS):
        out_codes[k] = message[k:k + 1, :]
    copies[6].wait()
    copies[7].wait()
    copies[8].wait()
    swap_rows_and_tiles(raster_in, turned)
    pl.semaphore_wait(barrier, OWNERS - 1 + 24 + 1)

    codes_sent = (tile, rep, out_codes, came, send_codes, recv_codes)
    came[tile] = out_codes[tile]
    send_some(other_owners(tile), *codes_sent)
    all_messages(*codes_sent).wait_recv()
    arrived = jnp.concatenate([came[k] for k in range(OWNERS)], axis=0)
    codes[...] = jnp.concatenate([arrived, pltpu.roll(arrived, 128 - 12, 1)], axis=0).T
    values_sent = (tile, rep, out_values, came_values, send_values, recv_values)
    send_ready, down_and_first, forward_rest, wait_rest, settle = add_up(
        (me, core, pair, mate, chip, level), packed, mate_in, paired, group_in, mine, level_in, whole, result, sems,
        lambda: pack_values(coded, out_values))
    form_terms(codes, beta_in, packed, coded, rows, turned, scaled, resid, send_ready)
    down_and_first(FIRST)

    def place_rows(part):
        values = values_of_fixes(value_bytes, lines[0, :, part * 128:(part + 1) * 128], slot_row[:, part * 128:(part + 1) * 128])
        own_rows[:, part * 128:(part + 1) * 128] = expand(values)

    peers = list(other_owners(tile))
    half = (FIRST + USED) // 2
    first_chores = [functools.partial(forward_rest, FIRST, half), functools.partial(forward_rest, half, USED)]
    first_chores += [functools.partial(send_some, peers[k:k + 21], *values_sent) for k in range(0, OWNERS - 1, 21)]
    first_chores += [functools.partial(wait_rest, FIRST)]

    def settle_all():
        settle()
        all_messages(*codes_sent).wait_send()
        came_values[tile] = out_values[tile]
        all_messages(*values_sent).wait_recv()

    chores = [settle_all]
    chores += [functools.partial(unpack_words, came_values, value_bytes, t) for t in range(3)]
    chores += [functools.partial(place_rows, part) for part in range(4)]
    solve_system(result, smooth_in, beta_new, system, spread, first_chores, chores)
    eta_new[...] = jnp.sum(dot(stacked_thirds(beta_new[...]), own_rows[...]), axis=0, keepdims=True)
    all_messages(*values_sent).wait_send()


def step(lines, raster, beta, smooth):
    f32, bf16, i32 = jnp.float32, jnp.bfloat16, jnp.int32
    one = pltpu.SemaphoreType.DMA
    group = pltpu.SemaphoreType.DMA((GROUP,))
    deep = pltpu.SemaphoreType.DMA((LEVELS,))
    chunks = pltpu.VMEM((GROUP, ROWS, 128), f32)
    chunk = pltpu.VMEM((ROWS, 128), f32)
    served = OWNERS * SLOTS
    return pl.pallas_call(
        step_kernel,
        out_shape=(jax.ShapeDtypeStruct((1, BASIS), f32), jax.ShapeDtypeStruct((1, FIXES), f32)),
        in_specs=[pl.BlockSpec(memory_space=pltpu.HBM)] * 9,
        out_specs=(VMEM, VMEM),
        scratch_shapes=[
            pltpu.VMEM((6, 1, FIXES), i32),
            pltpu.VMEM((16, LAYERS, 256), bf16),
            pltpu.VMEM((1, BASIS), f32),
            pltpu.SMEM((LAYERS,), f32),
            pltpu.VMEM((OWNERS, 1, 128), f32),
            pltpu.VMEM((OWNERS, 1, 128), f32),
            pltpu.VMEM((128, 128), f32),
            pltpu.VMEM((1024, 256), bf16),
            pltpu.VMEM((BASIS, served), bf16),
            pltpu.VMEM((BASIS, served), bf16),
            pltpu.VMEM((16, served), bf16),
            pltpu.VMEM((LAYERS, served), i32),
            pltpu.VMEM((2 * GROUP, ROWS, 128), f32),
            chunks, chunks, chunks,
            chunk,
            pltpu.VMEM((LEVELS, ROWS, 128), f32),
            chunk,
            pltpu.VMEM((2 * GROUP, ROWS, 128), f32),
            pltpu.VMEM((OWNERS, 6, 128), i32),
            pltpu.VMEM((OWNERS, 6, 128), i32),
            pltpu.VMEM((128, served), bf16),
            pltpu.VMEM((BASIS, FIXES), bf16),
            pltpu.VMEM((1, FIXES), f32),
            pltpu.VMEM((4, 128, BASIS + 128), f32),
            pltpu.VMEM((768, BASIS + 128), bf16),
            pltpu.SemaphoreType.DMA((9,)),
            one, one, one, one,
            one, group, one, one, deep, deep, one, group, one, group,
        ],
        compiler_params=pltpu.CompilerParams(collective_id=0, has_side_effects=True, vmem_limit_bytes=LIMIT),
    )(*lines, raster, beta, smooth)


def shards(owner, tile_local, anchor, frac_x, frac_y, label, raster, beta, smooth):
    lines = [array.reshape(1, FIXES) for array in (owner, tile_local, anchor, frac_x, frac_y, label)]
    beta_new, eta_new = step(lines, raster, beta.reshape(1, BASIS), smooth)
    return beta_new.reshape(BASIS), eta_new.reshape(FIXES)


def solution(mesh):
    fixes = P(("tile", "rep"))
    placed = (P(("tile", "rep"), None), fixes, fixes, fixes, fixes, fixes, P("tile", None, None), P(), P())
    return jax.shard_map(shards, mesh=mesh, in_specs=placed, out_specs=(P(), fixes), check_vma=False)
```
